512 devices in a mesh: basis: 128 (over z, x, y_lo, core), orb: 4 (over y_hi).
Axes of the slice: x: 4, y: 8 (y_hi: 4, y_lo: 2; y = y_hi * 2 + y_lo), z: 8, core: 2. Of those that a mesh axis runs over, the one named last changes fastest.
Arguments:
- coeffs: bfloat16 [32768, 1024], P('basis', 'orb'), may hold values from -6 to 6
- direction: bfloat16 [32768, 1024], P('basis', 'orb'), may hold values from -6 to 6
- ham_diag: bfloat16 [32768, 256], P('basis'), may hold values from -0.125 to 0.125
- ovl_diag: bfloat16 [32768, 256], P('basis'), may hold values from -0.0625 to 0.0625
- ham_band: bfloat16 [32768, 1024], P('basis'), may hold values from -0.125 to 0.125
- ovl_band: bfloat16 [32768, 1024], P('basis'), may hold values from -0.0625 to 0.0625
- band_mask: int32 [256, 8], P('basis'), may hold values 0 or 1
- local_mask: int32 [256, 8], P('basis', 'orb'), may hold values 0 or 1
Outputs:
- gradient: float32 [32768, 1024], P('basis', 'orb')
- line_terms: float32 [3, 1024], P(None, 'orb')
The draws below stay inside these ranges and needn't reach their ends.
All inputs are finite; a program needn't handle non-finite values. No bound on the sum of `band_mask` or of `local_mask` on one device may be relied on, other than what follows from the above.
Results may differ from the reference program's by a relative error of at most 0.0003.
Values may be sent and summed in bfloat16 or wider, within the bound.
No kernel may reach another device: no remote copies, remote signals or barrier semaphores. Data moves between devices by JAX's collectives and lax.ppermute only.
A program may use at most 64 MiB of HBM per device.

```python
import math
import jax
import jax.numpy as jnp
from jax import lax

BLK = 128
BASIS_DEV = 256
NORB = 1024
REACH = 4
NBAS = 32768
NBLK = 256
N_BASIS = 128


def set_ends(array, own_key, low, top_value):
    longest = array.shape.index(max(array.shape))
    spots = []
    for shift in (0, 1):
        where = [jax.random.randint(jax.random.fold_in(own_key, axis), (), 0, length) for axis, length in enumerate(array.shape)]
        where[longest] = (where[longest] + shift) % array.shape[longest]
        spots.append(tuple(where))
    return array.at[spots[0]].set(low).at[spots[1]].set(top_value)


def block_levels(stream_key, extent, cuts, low, top_value):
    def one(dim, parts):
        draws = jax.random.uniform(jax.random.fold_in(jax.random.fold_in(stream_key, 6), dim), (parts,), jnp.float32, low / len(cuts), top_value / len(cuts))
        return jnp.repeat(jnp.exp(draws), extent[dim] // parts).reshape((-1,) + (1,) * (len(extent) - dim - 1))

    factor_of = one(*cuts[0])
    for cut in cuts[1:]:
        factor_of = factor_of * one(*cut)
    return factor_of


def noise(own_key, extent, spread, limit, split=(), dtype=jnp.bfloat16):
    drawn = jax.random.normal(own_key, extent, jnp.float32) * spread
    if len(split) > 0:
        drawn = block_levels(own_key, extent, split, -0.22, 0.18) * drawn
    return jnp.clip(drawn, min=-limit, max=limit).astype(dtype)


def setup_inputs(seed: int = 0) -> dict:
    streams_of = jax.random.split(jax.random.key(seed), 9)
    coeffs = noise(streams_of[0], (NBAS, NORB), 1.0, 6.0, ((0, 128), (1, 4)))
    direction = noise(streams_of[1], (NBAS, NORB), 1.0, 6.0, ((0, 128), (1, 4)))
    ham_diag = noise(streams_of[2], (NBAS, BASIS_DEV), (BASIS_DEV * (2 * REACH + 2)) ** -0.5, 0.125, ((0, 128),))
    ovl_diag = noise(streams_of[3], (NBAS, BASIS_DEV), (4 * BASIS_DEV * (2 * REACH + 2)) ** -0.5, 0.0625, ((0, 128),))
    ham_band = noise(streams_of[4], (NBAS, REACH * BASIS_DEV), (BASIS_DEV * (2 * REACH + 2)) ** -0.5, 0.125, ((0, 128),))
    ovl_band = noise(streams_of[5], (NBAS, REACH * BASIS_DEV), (4 * BASIS_DEV * (2 * REACH + 2)) ** -0.5, 0.0625, ((0, 128),))
    band_mask = set_ends((jax.random.randint(streams_of[6], (NBLK, REACH * BASIS_DEV // BLK), 0, 4) < 3).astype(jnp.int32), jax.random.fold_in(streams_of[6], 1), 0, 1)
    local_mask = set_ends((jax.random.randint(streams_of[7], (NBLK, NORB // BLK), 0, 4) < 3).astype(jnp.int32), jax.random.fold_in(streams_of[7], 1), 0, 1)
    return dict(coeffs=coeffs, direction=direction, ham_diag=ham_diag, ovl_diag=ovl_diag, ham_band=ham_band, ovl_band=ovl_band, band_mask=band_mask, local_mask=local_mask)


def expand_mask(mask_blocks):
    grown = jnp.repeat(mask_blocks, BLK, axis=0)
    return jnp.repeat(grown, BLK, axis=1)

def batched(left, right):
    return jnp.einsum('dab,dbc->dac', left, right, precision=lax.Precision.HIGHEST)

def batched_left(left, right):
    return jnp.einsum('dba,dbc->dac', left, right, precision=lax.Precision.HIGHEST)

def reference(coeffs, direction, ham_diag, ovl_diag, ham_band, ovl_band, band_mask, local_mask):
    local_full = expand_mask(local_mask).astype(jnp.bfloat16)
    coeff = coeffs * local_full
    stacked = jnp.concatenate([coeff, direction], axis=1)
    runs = stacked.astype(jnp.float32).reshape(N_BASIS, BASIS_DEV, 2 * NORB)
    band_full = expand_mask(band_mask).astype(jnp.bfloat16)
    ham_tiles = (ham_band * band_full).astype(jnp.float32).reshape(N_BASIS, BASIS_DEV, REACH, BASIS_DEV)
    ovl_tiles = (ovl_band * band_full).astype(jnp.float32).reshape(N_BASIS, BASIS_DEV, REACH, BASIS_DEV)
    ham_d = ham_diag.astype(jnp.float32).reshape(N_BASIS, BASIS_DEV, BASIS_DEV)
    ovl_d = ovl_diag.astype(jnp.float32).reshape(N_BASIS, BASIS_DEV, BASIS_DEV)
    ham_x = batched(ham_d, runs) + batched_left(ham_d, runs)
    ovl_x = runs + batched(ovl_d, runs) + batched_left(ovl_d, runs)
    for step in range(REACH):
        ham_u = ham_tiles[:, :, step, :]
        ovl_v = ovl_tiles[:, :, step, :]
        ahead = jnp.roll(runs, -(step + 1), axis=0)
        ham_x = ham_x + batched(ham_u, ahead) + jnp.roll(batched_left(ham_u, runs), step + 1, axis=0)
        ovl_x = ovl_x + batched(ovl_v, ahead) + jnp.roll(batched_left(ovl_v, runs), step + 1, axis=0)
    ham_x = ham_x.reshape(NBAS, 2 * NORB)
    ovl_x = ovl_x.reshape(NBAS, 2 * NORB)
    ham_c, ham_dir = (ham_x[:, :NORB], ham_x[:, NORB:])
    ovl_c, ovl_dir = (ovl_x[:, :NORB], ovl_x[:, NORB:])
    grams = jnp.dot(coeff.astype(jnp.float32).T, jnp.concatenate([ham_c, ovl_c], axis=1), precision=lax.Precision.HIGHEST) / NBAS
    ham_gram, ovl_gram = (grams[:, :NORB], grams[:, NORB:])
    mixed = jnp.dot(ovl_c, ham_gram, precision=lax.Precision.HIGHEST) + jnp.dot(ham_c, ovl_gram, precision=lax.Precision.HIGHEST)
    gradient = (4.0 * ham_c - 2.0 * mixed) * local_full.astype(jnp.float32)
    dir_f = direction.astype(jnp.float32)
    scale = 1.0 / math.sqrt(NBAS)
    line_terms = jnp.stack([lax.optimization_barrier(jnp.sum(dir_f * ham_dir, axis=0)), lax.optimization_barrier(jnp.sum(dir_f * ovl_dir, axis=0)), lax.optimization_barrier(jnp.sum(dir_f * gradient, axis=0))], axis=0) * scale
    return (gradient, line_terms)
```

```python
import math

import jax
import jax.numpy as jnp
from jax import lax
from jax.sharding import Mesh, PartitionSpec as P

BLK = 128
BASIS = ("z", "x", "y", "c")
CHIPS = ("z", "x", "y")


def shifted(shard, by):
    count = lax.axis_size(BASIS)
    return lax.ppermute(shard, BASIS, [(i, (i + by) % count) for i in range(count)])


def swap_core(shard):
    return lax.ppermute(shard, "c", [(0, 1), (1, 0)])


def expand_mask(mask_blocks):
    grown = jnp.repeat(mask_blocks, BLK, axis=0)
    return jnp.repeat(grown, BLK, axis=1)


def plain_dot(left, right):
    return jnp.dot(left, right, preferred_element_type=jnp.float32)


def dot_left(left, right, precision=None):
    return lax.dot_general(
        left, right, (((0,), (0,)), ((), ())),
        precision=precision, preferred_element_type=jnp.float32,
    )


def summed_shares(rows):
    half = rows.shape[0] // 2
    core = lax.axis_index("c")
    mine = lax.dynamic_slice_in_dim(rows, core * half, half, 0)
    other = lax.dynamic_slice_in_dim(rows, (1 - core) * half, half, 0)
    pair = mine + swap_core(other)
    chips = lax.axis_size(CHIPS)
    parts = lax.all_to_all(pair.reshape(chips, half // chips, rows.shape[1]), CHIPS, 0, 0)
    return jnp.sum(parts, axis=0)


def gathered_shares(share):
    chips = lax.axis_size(CHIPS)
    copies = jnp.broadcast_to(share[None], (chips,) + share.shape)
    half = lax.all_to_all(copies, CHIPS, 0, 0).reshape(chips * share.shape[0], share.shape[1])
    other = swap_core(half)
    core = lax.axis_index("c")
    first = jnp.where(core == 0, half, other)
    second = jnp.where(core == 0, other, half)
    return jnp.concatenate([first, second], axis=0)


def on_device(coeffs, direction, ham_diag, ovl_diag, ham_band, ovl_band, band_mask, local_mask):
    rows = coeffs.shape[0]
    cols = coeffs.shape[1]
    reach = ham_band.shape[1] // rows
    orbs = lax.axis_size("orb")
    basis_total = rows * lax.axis_size(BASIS)
    local_full = expand_mask(local_mask).astype(jnp.bfloat16)
    coeff = coeffs * local_full
    stacked = jnp.concatenate([coeff, direction], axis=1)
    band_full = expand_mask(band_mask).astype(jnp.bfloat16)
    ham_tiles = ham_band * band_full
    ovl_tiles = ovl_band * band_full

    ahead, behind = [], []
    for step in range(1, reach + 1):
        part = slice((step - 1) * rows, step * rows)
        sent = jnp.concatenate([coeff, ham_tiles[:, part], ovl_tiles[:, part]], axis=1)
        behind.append(shifted(sent, step))
        ahead.append(shifted(stacked, -step))
    peers = [
        lax.ppermute(coeff, "orb", [(i, (i + by) % orbs) for i in range(orbs)])
        for by in range(1, orbs)
    ]

    forward = plain_dot(jnp.concatenate([ham_diag, ovl_diag], axis=0), stacked)
    for step in range(reach):
        part = slice(step * rows, (step + 1) * rows)
        tiles = jnp.concatenate([ham_tiles[:, part], ovl_tiles[:, part]], axis=0)
        forward = forward + plain_dot(tiles, ahead[step])
    back = dot_left(jnp.concatenate([ham_diag, ovl_diag], axis=1), coeff)
    for got in behind:
        back = back + dot_left(got[:, cols:], got[:, :cols])
    ham_c = forward[:rows, :cols] + back[:rows]
    ovl_c = forward[rows:, :cols] + back[rows:] + coeff.astype(jnp.float32)

    dir_f = direction.astype(jnp.float32)
    ham_line = 2.0 * jnp.sum(dir_f * forward[:rows, cols:], axis=0)
    ovl_line = jnp.sum(dir_f * (2.0 * forward[rows:, cols:] + dir_f), axis=0)

    both_c = jnp.concatenate([ham_c, ovl_c], axis=1)
    every_c = lax.all_gather(both_c, "orb", axis=0)

    place = lax.axis_index("orb")
    partial = []
    for by, held in enumerate([coeff] + peers):
        partial.append(dot_left(held.astype(jnp.float32), both_c, lax.Precision.HIGH))
    partial = jnp.stack(partial, axis=0)
    share = summed_shares(partial.reshape(orbs * cols, 2 * cols))
    grams = gathered_shares(share) * (1.0 / basis_total)
    grams = grams.reshape(orbs, cols, 2 * cols)

    mixed = jnp.zeros((rows, cols), jnp.float32)
    for by in range(orbs):
        theirs = lax.dynamic_index_in_dim(every_c, (place - by) % orbs, 0, keepdims=False)
        mixed = mixed + jnp.dot(theirs[:, cols:], grams[by, :, :cols], precision=lax.Precision.HIGH)
        mixed = mixed + jnp.dot(theirs[:, :cols], grams[by, :, cols:], precision=lax.Precision.HIGH)
    gradient = (4.0 * ham_c - 2.0 * mixed) * local_full.astype(jnp.float32)
    grad_line = jnp.sum(dir_f * gradient, axis=0)
    lines = jnp.stack([ham_line, ovl_line, grad_line], axis=0)
    devices = lax.axis_size(BASIS)
    copies = jnp.broadcast_to(lines.reshape(1, -1, BLK), (devices, lines.size // BLK, BLK))
    every_line = lax.all_to_all(copies, BASIS, 0, 0)
    line_terms = jnp.sum(every_line, axis=0).reshape(lines.shape) * (1.0 / math.sqrt(basis_total))
    return (gradient, line_terms)


def solution(mesh):
    fine = Mesh(mesh.devices.reshape(8, 4, 2, 2, 4), BASIS + ("orb",))
    placed = (P(BASIS, "orb"), P(BASIS, "orb")) + (P(BASIS, None),) * 5 + (P(BASIS, "orb"),)
    return jax.shard_map(
        on_device,
        mesh=fine,
        in_specs=placed,
        out_specs=(P(BASIS, "orb"), P(None, "orb")),
        check_vma=False,
    )
```

```python
import math

import jax
import jax.numpy as jnp
from jax import lax
from jax.sharding import Mesh, PartitionSpec as P

BLK = 128
BASIS = ("z", "x", "y", "c")
SIZES = {"z": 8, "x": 4, "y": 2, "c": 2, "orb": 4}
HIGH = lax.Precision.HIGH


def shifted(shard, by):
    count = lax.axis_size(BASIS)
    return lax.ppermute(shard, BASIS, [(i, (i + by) % count) for i in range(count)])


def swapped(shard, axis):
    return lax.ppermute(shard, axis, [(0, 1), (1, 0)])


def expand_mask(mask_blocks):
    grown = jnp.repeat(mask_blocks, BLK, axis=0)
    return jnp.repeat(grown, BLK, axis=1)


def plain_dot(left, right, precision=None):
    return jnp.dot(left, right, precision=precision, preferred_element_type=jnp.float32)


def dot_left(left, right, precision=None):
    return lax.dot_general(
        left, right, (((0,), (0,)), ((), ())),
        precision=precision, preferred_element_type=jnp.float32,
    )


def sent_over(shard, axes, target):
    sizes = [SIZES[a] for a in axes]
    count = math.prod(sizes)
    pairs = []
    for source in range(count):
        rest, coords = source, []
        for size in reversed(sizes):
            coords.append(rest % size)
            rest //= size
        goal = target(*reversed(coords))
        if goal is not None:
            index = 0
            for size, coord in zip(sizes, goal):
                index = index * size + coord
            pairs.append((source, index))
    return lax.ppermute(shard, axes, pairs)


def on_device(coeffs, direction, ham_diag, ovl_diag, ham_band, ovl_band, band_mask, local_mask):
    rows = coeffs.shape[0]
    cols = coeffs.shape[1]
    basis_total = rows * lax.axis_size(BASIS)
    core = lax.axis_index("c")
    first_core = core == 0
    local_full = expand_mask(local_mask).astype(jnp.bfloat16)
    coeff = coeffs * local_full
    stacked = jnp.concatenate([coeff, direction], axis=1)
    band_full = expand_mask(band_mask).astype(jnp.bfloat16)
    ham_tiles = ham_band * band_full
    ovl_tiles = ovl_band * band_full

    def tile(step):
        part = slice((step - 1) * rows, step * rows)
        return jnp.concatenate([ham_tiles[:, part], ovl_tiles[:, part]], axis=1)

    ahead_2 = shifted(stacked, -2)
    ahead_4 = shifted(stacked, -4)
    spare = jnp.where(first_core, tile(3), tile(1))
    behind_2 = shifted(jnp.concatenate([coeff, spare, tile(2)], axis=1), 2)
    behind_4 = shifted(jnp.concatenate([coeff, tile(3), tile(4)], axis=1), 4)
    peer_a = sent_over(coeff, ("c", "orb"), lambda c, o: (0, o) if c else (1, o ^ 2))
    peer_b = sent_over(coeff, ("c", "orb"), lambda c, o: (0, o ^ 1) if c else (1, o ^ 3))
    peer_c = sent_over(coeff, ("c", "orb"), lambda c, o: (1, o ^ 2) if c else (0, o ^ 1))
    peer_d = sent_over(coeff, ("c", "orb"), lambda c, o: (1, o ^ 3) if c else None)
    gram_left = jnp.concatenate(
        [
            jnp.concatenate(
                [jnp.where(first_core, coeff, peer_c), jnp.where(first_core, peer_c, peer_d)], axis=1
            ),
            jnp.concatenate([peer_a, peer_b], axis=1),
        ],
        axis=0,
    )
    odd_ahead = swapped(
        jnp.where(
            first_core,
            jnp.concatenate([ahead_2, ahead_4], axis=1),
            jnp.concatenate([stacked, ahead_2], axis=1),
        ),
        "c",
    )
    pack = cols + 2 * rows
    odd_behind = swapped(
        jnp.where(
            first_core,
            jnp.concatenate([coeff, tile(1), behind_2[:, :pack]], axis=1),
            jnp.concatenate([behind_2[:, :pack], behind_4[:, :pack]], axis=1),
        ),
        "c",
    )
    dir_mine = direction * local_full
    dir_runs = [dir_mine] + [
        sent_over(dir_mine, ("y", "c"), lambda y, c, j=j: (y ^ (j >> 1), c ^ (j & 1)))
        for j in range(1, 4)
    ]

    def upright(step):
        part = slice((step - 1) * rows, step * rows)
        return jnp.concatenate([ham_tiles[:, part], ovl_tiles[:, part]], axis=0)

    forward = plain_dot(jnp.concatenate([ham_diag, ovl_diag], axis=0), stacked)
    forward = forward + plain_dot(upright(2), ahead_2)
    forward = forward + plain_dot(upright(4), ahead_4)
    forward = forward + plain_dot(upright(1), odd_ahead[:, : 2 * cols])
    forward = forward + plain_dot(upright(3), odd_ahead[:, 2 * cols :])
    back = dot_left(jnp.concatenate([ham_diag, ovl_diag], axis=1), coeff)
    back = back + dot_left(behind_2[:, pack:], behind_2[:, :cols])
    back = back + dot_left(behind_4[:, pack:], behind_4[:, :cols])
    back = back + dot_left(odd_behind[:, cols:pack], odd_behind[:, :cols])
    back = back + dot_left(odd_behind[:, pack + cols :], odd_behind[:, pack : pack + cols])
    ham_c = forward[:rows, :cols] + back[:rows]
    ovl_c = forward[rows:, :cols] + back[rows:] + coeff.astype(jnp.float32)
    both_c = jnp.concatenate([ham_c, ovl_c], axis=1)

    dir_f = direction.astype(jnp.float32)
    ham_line = 2.0 * jnp.sum(dir_f * forward[:rows, cols:], axis=0)
    ovl_line = jnp.sum(dir_f * (2.0 * forward[rows:, cols:] + dir_f), axis=0)

    other_c = swapped(both_c, "c")
    runs = []
    for j in range(4):
        def target(y, c, o, j=j):
            y, c = y ^ (j >> 1), c ^ (j & 1)
            return (y, c, o ^ (2 * c + y))
        runs.append(sent_over(both_c, ("y", "c", "orb"), target))

    partial = dot_left(
        gram_left.astype(jnp.float32), jnp.concatenate([both_c, other_c], axis=0), HIGH
    )
    chips = lax.axis_size(("y", "z", "x"))
    parts = lax.all_to_all(
        partial.reshape(chips, 2 * cols // chips, 2 * cols), ("y", "z", "x"), 0, 0
    )
    strip = jnp.sum(parts, axis=0) * (1.0 / basis_total)
    strips = lax.axis_size(("z", "x"))
    block = lax.all_to_all(
        jnp.broadcast_to(strip[None], (strips,) + strip.shape), ("z", "x"), 0, 0
    ).reshape(cols, 2 * cols)

    mixed = plain_dot(
        jnp.concatenate(runs, axis=0),
        jnp.concatenate([block[:, cols:], block[:, :cols]], axis=0),
        HIGH,
    ).reshape(4, rows, cols)

    grad_line = 4.0 * jnp.sum(dir_mine.astype(jnp.float32) * ham_c, axis=0)
    for j in range(4):
        grad_line = grad_line - 2.0 * jnp.sum(dir_runs[j].astype(jnp.float32) * mixed[j], axis=0)
    lines = jnp.stack([ham_line, ovl_line, grad_line], axis=0)
    lines = lines + swapped(lines, "c")
    copies = jnp.broadcast_to(lines.reshape(1, -1, BLK), (chips, lines.size // BLK, BLK))
    every_line = lax.all_to_all(copies, ("z", "x", "y"), 0, 0)
    line_terms = jnp.sum(every_line, axis=0).reshape(lines.shape) * (1.0 / math.sqrt(basis_total))

    crossed = swapped(jnp.concatenate([mixed[1], mixed[3]], axis=1), "c")
    near = mixed[0] + crossed[:, :cols]
    far = mixed[2] + crossed[:, cols:]
    total = near + swapped(far, "y")
    gradient = (4.0 * ham_c - 2.0 * total) * local_full.astype(jnp.float32)
    return (gradient, line_terms)


def solution(mesh):
    fine = Mesh(mesh.devices.reshape(tuple(SIZES.values())), tuple(SIZES))
    placed = (P(BASIS, "orb"), P(BASIS, "orb")) + (P(BASIS, None),) * 5 + (P(BASIS, "orb"),)
    return jax.shard_map(
        on_device,
        mesh=fine,
        in_specs=placed,
        out_specs=(P(BASIS, "orb"), P(None, "orb")),
        check_vma=False,
    )
```

```python
import math

import jax
import jax.numpy as jnp
from jax import lax
from jax.experimental import pallas as pl
from jax.sharding import Mesh, PartitionSpec as P

BLK = 128
BASIS = ("z", "x", "y", "c")
SIZES = {"z": 8, "x": 4, "y": 2, "c": 2, "orb": 4}
HIGH = lax.Precision.HIGH


def shifted(shard, by):
    count = lax.axis_size(BASIS)
    return lax.ppermute(shard, BASIS, [(i, (i + by) % count) for i in range(count)])


def swapped(shard, axis):
    return lax.ppermute(shard, axis, [(0, 1), (1, 0)])


def expand_mask(mask_blocks):
    grown = jnp.repeat(mask_blocks, BLK, axis=0)
    return jnp.repeat(grown, BLK, axis=1)


def plain_dot(left, right, precision=None):
    return jnp.dot(left, right, precision=precision, preferred_element_type=jnp.float32)


def dot_left(left, right, precision=None):
    return lax.dot_general(
        left, right, (((0,), (0,)), ((), ())),
        precision=precision, preferred_element_type=jnp.float32,
    )


def sent_over(shard, axes, target):
    sizes = [SIZES[a] for a in axes]
    count = math.prod(sizes)
    pairs = []
    for source in range(count):
        rest, coords = source, []
        for size in reversed(sizes):
            coords.append(rest % size)
            rest //= size
        goal = target(*reversed(coords))
        if goal is not None:
            index = 0
            for size, coord in zip(sizes, goal):
                index = index * size + coord
            pairs.append((source, index))
    return lax.ppermute(shard, axes, pairs)


def after(shard, *others):
    def nothing(*refs):
        del refs

    return pl.pallas_call(
        nothing,
        out_shape=jax.ShapeDtypeStruct(shard.shape, shard.dtype),
        in_specs=[pl.BlockSpec(memory_space=pl.ANY)] * (1 + len(others)),
        out_specs=pl.BlockSpec(memory_space=pl.ANY),
        input_output_aliases={0: 0},
    )(shard, *others)


def on_device(coeffs, direction, ham_diag, ovl_diag, ham_band, ovl_band, band_mask, local_mask):
    rows = coeffs.shape[0]
    cols = coeffs.shape[1]
    basis_total = rows * lax.axis_size(BASIS)
    core = lax.axis_index("c")
    first_core = core == 0
    local_full = expand_mask(local_mask).astype(jnp.bfloat16)
    coeff = coeffs * local_full
    stacked = jnp.concatenate([coeff, direction], axis=1)
    band_full = expand_mask(band_mask).astype(jnp.bfloat16)
    ham_tiles = ham_band * band_full
    ovl_tiles = ovl_band * band_full

    def tile(step):
        part = slice((step - 1) * rows, step * rows)
        return jnp.concatenate([ham_tiles[:, part], ovl_tiles[:, part]], axis=1)

    ahead_2 = shifted(stacked, -2)
    ahead_4 = shifted(stacked, -4)
    spare = jnp.where(first_core, tile(3), tile(1))
    behind_2 = shifted(jnp.concatenate([coeff, spare, tile(2)], axis=1), 2)
    behind_4 = shifted(jnp.concatenate([coeff, tile(3), tile(4)], axis=1), 4)
    sent_coeff = after(coeff, ahead_2)
    peer_a = sent_over(sent_coeff, ("c", "orb"), lambda c, o: (0, o) if c else (1, o ^ 2))
    peer_b = sent_over(sent_coeff, ("c", "orb"), lambda c, o: (0, o ^ 1) if c else (1, o ^ 3))
    peer_c = sent_over(sent_coeff, ("c", "orb"), lambda c, o: (1, o ^ 2) if c else (0, o ^ 1))
    peer_d = sent_over(sent_coeff, ("c", "orb"), lambda c, o: (1, o ^ 3) if c else None)
    gram_left = jnp.concatenate(
        [
            jnp.concatenate(
                [jnp.where(first_core, coeff, peer_c), jnp.where(first_core, peer_c, peer_d)], axis=1
            ),
            jnp.concatenate([peer_a, peer_b], axis=1),
        ],
        axis=0,
    )
    odd_ahead = swapped(
        jnp.where(
            first_core,
            jnp.concatenate([ahead_2, ahead_4], axis=1),
            jnp.concatenate([stacked, ahead_2], axis=1),
        ),
        "c",
    )
    pack = cols + 2 * rows
    behind_pack = jnp.where(
        first_core,
        jnp.concatenate([coeff, tile(1), behind_2[:, :pack]], axis=1),
        jnp.concatenate([behind_2[:, :pack], behind_4[:, :pack]], axis=1),
    )
    odd_behind = swapped(after(behind_pack, peer_a, peer_b, peer_c, peer_d), "c")
    dir_mine = direction * local_full
    dir_far = swapped(dir_mine, "y")

    def upright(step):
        part = slice((step - 1) * rows, step * rows)
        return jnp.concatenate([ham_tiles[:, part], ovl_tiles[:, part]], axis=0)

    forward = plain_dot(jnp.concatenate([ham_diag, ovl_diag], axis=0), stacked)
    forward = forward + plain_dot(upright(2), ahead_2)
    forward = forward + plain_dot(upright(4), ahead_4)
    forward = forward + plain_dot(upright(1), odd_ahead[:, : 2 * cols])
    forward = forward + plain_dot(upright(3), odd_ahead[:, 2 * cols :])
    back = dot_left(jnp.concatenate([ham_diag, ovl_diag], axis=1), coeff)
    back = back + dot_left(behind_2[:, pack:], behind_2[:, :cols])
    back = back + dot_left(behind_4[:, pack:], behind_4[:, :cols])
    back = back + dot_left(odd_behind[:, cols:pack], odd_behind[:, :cols])
    back = back + dot_left(odd_behind[:, pack + cols :], odd_behind[:, pack : pack + cols])
    ham_c = forward[:rows, :cols] + back[:rows]
    ovl_c = forward[rows:, :cols] + back[rows:] + coeff.astype(jnp.float32)
    both_c = jnp.concatenate([ham_c, ovl_c], axis=1)

    dir_f = direction.astype(jnp.float32)
    ham_line = 2.0 * jnp.sum(dir_f * forward[:rows, cols:], axis=0)
    ovl_line = jnp.sum(dir_f * (2.0 * forward[rows:, cols:] + dir_f), axis=0)

    other_c = swapped(both_c, "c")
    chip = lax.axis_index("y")
    right = jnp.concatenate([both_c, other_c], axis=0)
    left_mine = jnp.where(chip == 0, gram_left[:, :cols], gram_left[:, cols:]).astype(jnp.float32)
    left_far = jnp.where(chip == 0, gram_left[:, cols:], gram_left[:, :cols]).astype(jnp.float32)
    partial_far = dot_left(left_far, right, HIGH)
    sent_c = after(both_c, partial_far)
    runs = []
    for j in range(4):
        def target(y, c, o, j=j):
            y, c = y ^ (j >> 1), c ^ (j & 1)
            return (y, c, o ^ (2 * c + y))
        runs.append(sent_over(sent_c, ("y", "c", "orb"), target))
    partial = dot_left(left_mine, right, HIGH) + swapped(partial_far, "y")
    strips = lax.axis_size(("z", "x"))
    parts = lax.all_to_all(partial.reshape(strips, cols // strips, 2 * cols), ("z", "x"), 0, 0)
    strip = jnp.sum(parts, axis=0) * (1.0 / basis_total)
    strip = after(strip, dir_far, *runs)
    block = lax.all_to_all(
        jnp.broadcast_to(strip[None], (strips,) + strip.shape), ("z", "x"), 0, 0
    ).reshape(cols, 2 * cols)

    mixed = plain_dot(
        jnp.concatenate(runs, axis=0),
        jnp.concatenate([block[:, cols:], block[:, :cols]], axis=0),
        HIGH,
    ).reshape(4, rows, cols)

    crossed = swapped(jnp.concatenate([mixed[1], mixed[3]], axis=1), "c")
    near = mixed[0] + crossed[:, :cols]
    far = mixed[2] + crossed[:, cols:]
    total = near + swapped(far, "y")
    gradient = (4.0 * ham_c - 2.0 * total) * local_full.astype(jnp.float32)

    grad_line = jnp.sum(
        dir_mine.astype(jnp.float32) * (4.0 * ham_c - 2.0 * near)
        - dir_far.astype(jnp.float32) * (2.0 * far),
        axis=0,
    )
    lines = jnp.stack([ham_line, ovl_line, grad_line], axis=0)
    lines = lines + swapped(lines, "c")
    chips = lax.axis_size(("z", "x", "y"))
    copies = jnp.broadcast_to(lines.reshape(1, -1, BLK), (chips, lines.size // BLK, BLK))
    every_line = lax.all_to_all(copies, ("z", "x", "y"), 0, 0)
    line_terms = jnp.sum(every_line, axis=0).reshape(lines.shape) * (1.0 / math.sqrt(basis_total))
    return (gradient, line_terms)


def solution(mesh):
    fine = Mesh(mesh.devices.reshape(tuple(SIZES.values())), tuple(SIZES))
    placed = (P(BASIS, "orb"), P(BASIS, "orb")) + (P(BASIS, None),) * 5 + (P(BASIS, "orb"),)
    return jax.shard_map(
        on_device,
        mesh=fine,
        in_specs=placed,
        out_specs=(P(BASIS, "orb"), P(None, "orb")),
        check_vma=False,
    )
```

```python
import math

import jax
import jax.numpy as jnp
from jax import lax
from jax.sharding import Mesh, PartitionSpec as P

BLK = 128
BASIS = ("z", "x", "y", "c")
SIZES = {"z": 8, "x": 4, "y": 2, "c": 2, "orb": 4}
HIGH = lax.Precision.HIGH


def shifted(shard, by):
    count = lax.axis_size(BASIS)
    return lax.ppermute(shard, BASIS, [(i, (i + by) % count) for i in range(count)])


def swapped(shard, axis):
    return lax.ppermute(shard, axis, [(0, 1), (1, 0)])


def expand_mask(mask_blocks):
    grown = jnp.repeat(mask_blocks, BLK, axis=0)
    return jnp.repeat(grown, BLK, axis=1)


def plain_dot(left, right, precision=None):
    return jnp.dot(left, right, precision=precision, preferred_element_type=jnp.float32)


def dot_left(left, right, precision=None):
    return lax.dot_general(
        left, right, (((0,), (0,)), ((), ())),
        precision=precision, preferred_element_type=jnp.float32,
    )


def on_device(coeffs, direction, ham_diag, ovl_diag, ham_band, ovl_band, band_mask, local_mask):
    rows = coeffs.shape[0]
    cols = coeffs.shape[1]
    basis_total = rows * lax.axis_size(BASIS)
    core = lax.axis_index("c")
    first_core = core == 0
    local_full = expand_mask(local_mask).astype(jnp.bfloat16)
    coeff = coeffs * local_full
    stacked = jnp.concatenate([coeff, direction], axis=1)
    band_full = expand_mask(band_mask).astype(jnp.bfloat16)
    ham_tiles = ham_band * band_full
    ovl_tiles = ovl_band * band_full

    def tile(step):
        part = slice((step - 1) * rows, step * rows)
        return jnp.concatenate([ham_tiles[:, part], ovl_tiles[:, part]], axis=1)

    ahead_2 = shifted(stacked, -2)
    ahead_4 = shifted(stacked, -4)
    spare = jnp.where(first_core, tile(3), tile(1))
    behind_2 = shifted(jnp.concatenate([coeff, spare, tile(2)], axis=1), 2)
    behind_4 = shifted(jnp.concatenate([coeff, tile(3), tile(4)], axis=1), 4)
    peers = [coeff] + [
        lax.ppermute(coeff, "orb", [(i, i ^ g) for i in range(4)]) for g in range(1, 4)
    ]
    pack = cols + 2 * rows
    crossing = jnp.where(
        first_core,
        jnp.concatenate(
            [coeff, tile(1), behind_2[:, :pack], ahead_2, ahead_4, peers[2], peers[3]], axis=1
        ),
        jnp.concatenate(
            [behind_2[:, :pack], behind_4[:, :pack], stacked, ahead_2, coeff, peers[1]], axis=1
        ),
    )
    crossed = swapped(crossing, "c")
    odd_behind = crossed[:, : 2 * pack]
    odd_ahead = crossed[:, 2 * pack : 2 * pack + 4 * cols]
    gram_left = jnp.concatenate(
        [
            jnp.where(
                first_core,
                jnp.concatenate(peers[:2], axis=1),
                jnp.concatenate(peers[2:], axis=1),
            ),
            crossed[:, 2 * pack + 4 * cols :],
        ],
        axis=0,
    )

    def upright(step):
        part = slice((step - 1) * rows, step * rows)
        return jnp.concatenate([ham_tiles[:, part], ovl_tiles[:, part]], axis=0)

    forward = plain_dot(jnp.concatenate([ham_diag, ovl_diag], axis=0), stacked)
    forward = forward + plain_dot(upright(2), ahead_2)
    forward = forward + plain_dot(upright(4), ahead_4)
    forward = forward + plain_dot(upright(1), odd_ahead[:, : 2 * cols])
    forward = forward + plain_dot(upright(3), odd_ahead[:, 2 * cols :])
    back = dot_left(jnp.concatenate([ham_diag, ovl_diag], axis=1), coeff)
    back = back + dot_left(behind_2[:, pack:], behind_2[:, :cols])
    back = back + dot_left(behind_4[:, pack:], behind_4[:, :cols])
    back = back + dot_left(odd_behind[:, cols:pack], odd_behind[:, :cols])
    back = back + dot_left(odd_behind[:, pack + cols :], odd_behind[:, pack : pack + cols])
    ham_c = forward[:rows, :cols] + back[:rows]
    ovl_c = forward[rows:, :cols] + back[rows:] + coeff.astype(jnp.float32)
    both_c = jnp.concatenate([ham_c, ovl_c], axis=1)

    dir_f = direction.astype(jnp.float32)
    ham_line = 2.0 * jnp.sum(dir_f * forward[:rows, cols:], axis=0)
    ovl_line = jnp.sum(dir_f * (2.0 * forward[rows:, cols:] + dir_f), axis=0)

    every_c = lax.all_gather(both_c, "orb", axis=0)
    other_c = swapped(both_c, "c")
    place = lax.axis_index("orb")

    def group(g):
        theirs = lax.dynamic_index_in_dim(every_c, place ^ g, 0, keepdims=False)
        return jnp.concatenate([theirs[:, cols:], theirs[:, :cols]], axis=1)

    partial = dot_left(
        gram_left.astype(jnp.float32), jnp.concatenate([both_c, other_c], axis=0), HIGH
    )
    chip_axes = ("y", "z", "x")
    chips = lax.axis_size(chip_axes)
    parts = lax.all_to_all(
        partial.reshape(chips, 2 * cols // chips, 2 * cols), chip_axes, 0, 0
    )
    strip = jnp.sum(parts, axis=0) * (1.0 / basis_total)
    half = lax.all_to_all(
        jnp.broadcast_to(strip[None], (chips,) + strip.shape), chip_axes, 0, 0
    ).reshape(2, cols, 2 * cols)
    other_half = swapped(half, "c")
    mixed = jnp.zeros((rows, cols), jnp.float32)
    for base, grams in ((2 * core, half), (2 - 2 * core, other_half)):
        for k in range(2):
            theirs = group(base + k)
            mixed = mixed + plain_dot(theirs[:, :cols], grams[k, :, :cols], HIGH)
            mixed = mixed + plain_dot(theirs[:, cols:], grams[k, :, cols:], HIGH)
    gradient = (4.0 * ham_c - 2.0 * mixed) * local_full.astype(jnp.float32)

    lines = jnp.stack([ham_line, ovl_line, jnp.sum(dir_f * gradient, axis=0)], axis=0)
    lines = lines + swapped(lines, "c")
    copies = jnp.broadcast_to(lines.reshape(1, -1, BLK), (chips, lines.size // BLK, BLK))
    every_line = lax.all_to_all(copies, chip_axes, 0, 0)
    line_terms = jnp.sum(every_line, axis=0).reshape(lines.shape) * (1.0 / math.sqrt(basis_total))
    return (gradient, line_terms)


def solution(mesh):
    fine = Mesh(mesh.devices.reshape(tuple(SIZES.values())), tuple(SIZES))
    placed = (P(BASIS, "orb"), P(BASIS, "orb")) + (P(BASIS, None),) * 5 + (P(BASIS, "orb"),)
    return jax.shard_map(
        on_device,
        mesh=fine,
        in_specs=placed,
        out_specs=(P(BASIS, "orb"), P(None, "orb")),
        check_vma=False,
    )
```

```python
import math

import jax
import jax.numpy as jnp
from jax import lax
from jax.experimental import pallas as pl
from jax.sharding import Mesh, PartitionSpec as P

BLK = 128
BASIS = ("z", "x", "y", "c")
SIZES = {"z": 8, "x": 4, "y": 2, "c": 2, "orb": 4}
HIGH = lax.Precision.HIGH


def shifted(shard, by):
    count = lax.axis_size(BASIS)
    return lax.ppermute(shard, BASIS, [(i, (i + by) % count) for i in range(count)])


def swapped(shard, axis):
    return lax.ppermute(shard, axis, [(0, 1), (1, 0)])


def expand_mask(mask_blocks):
    grown = jnp.repeat(mask_blocks, BLK, axis=0)
    return jnp.repeat(grown, BLK, axis=1)


def plain_dot(left, right, precision=None):
    return jnp.dot(left, right, precision=precision, preferred_element_type=jnp.float32)


def dot_left(left, right, precision=None):
    return lax.dot_general(
        left, right, (((0,), (0,)), ((), ())),
        precision=precision, preferred_element_type=jnp.float32,
    )


def after(shard, *others):
    def nothing(*refs):
        del refs

    return pl.pallas_call(
        nothing,
        out_shape=jax.ShapeDtypeStruct(shard.shape, shard.dtype),
        in_specs=[pl.BlockSpec(memory_space=pl.ANY)] * (1 + len(others)),
        out_specs=pl.BlockSpec(memory_space=pl.ANY),
        input_output_aliases={0: 0},
    )(shard, *others)


def over_orb(shard, g):
    return lax.ppermute(shard, "orb", [(i, i ^ g) for i in range(SIZES["orb"])])


def on_device(coeffs, direction, ham_diag, ovl_diag, ham_band, ovl_band, band_mask, local_mask):
    rows = coeffs.shape[0]
    cols = coeffs.shape[1]
    basis_total = rows * lax.axis_size(BASIS)
    core = lax.axis_index("c")
    first_core = core == 0
    local_full = expand_mask(local_mask).astype(jnp.bfloat16)
    coeff = coeffs * local_full
    stacked = jnp.concatenate([coeff, direction], axis=1)
    band_full = expand_mask(band_mask).astype(jnp.bfloat16)
    ham_tiles = ham_band * band_full
    ovl_tiles = ovl_band * band_full

    def tile(step):
        part = slice((step - 1) * rows, step * rows)
        return jnp.concatenate([ham_tiles[:, part], ovl_tiles[:, part]], axis=1)

    ahead_2 = shifted(stacked, -2)
    ahead_4 = shifted(stacked, -4)
    spare = jnp.where(first_core, tile(3), tile(1))
    behind_2 = shifted(jnp.concatenate([coeff, spare, tile(2)], axis=1), 2)
    behind_4 = shifted(jnp.concatenate([coeff, tile(3), tile(4)], axis=1), 4)
    place = lax.axis_index("orb")
    every_coeff = lax.all_to_all(
        jnp.broadcast_to(after(coeff, stacked)[None], (SIZES["orb"], rows, cols)), "orb", 0, 0
    )

    def peer(g):
        return lax.dynamic_index_in_dim(every_coeff, place ^ g, 0, keepdims=False)

    near_peers = [peer(2 * core + k) for k in range(2)]
    far_peers = [peer(2 - 2 * core + k) for k in range(2)]
    pack = cols + 2 * rows
    crossing = jnp.where(
        first_core,
        jnp.concatenate(
            [coeff, tile(1), behind_2[:, :pack], ahead_2, ahead_4] + far_peers, axis=1
        ),
        jnp.concatenate(
            [behind_2[:, :pack], behind_4[:, :pack], stacked, ahead_2] + far_peers, axis=1
        ),
    )
    crossed = swapped(crossing, "c")
    odd_behind = crossed[:, : 2 * pack]
    odd_ahead = crossed[:, 2 * pack : 2 * pack + 4 * cols]
    gram_left = jnp.concatenate(
        [
            jnp.concatenate(near_peers, axis=1),
            crossed[:, 2 * pack + 4 * cols :],
        ],
        axis=0,
    )

    def upright(step):
        part = slice((step - 1) * rows, step * rows)
        return jnp.concatenate([ham_tiles[:, part], ovl_tiles[:, part]], axis=0)

    forward = plain_dot(jnp.concatenate([ham_diag, ovl_diag], axis=0), stacked)
    forward = forward + plain_dot(upright(2), ahead_2)
    forward = forward + plain_dot(upright(4), ahead_4)
    forward = forward + plain_dot(upright(1), odd_ahead[:, : 2 * cols])
    forward = forward + plain_dot(upright(3), odd_ahead[:, 2 * cols :])
    back = dot_left(jnp.concatenate([ham_diag, ovl_diag], axis=1), coeff)
    back = back + dot_left(behind_2[:, pack:], behind_2[:, :cols])
    back = back + dot_left(behind_4[:, pack:], behind_4[:, :cols])
    back = back + dot_left(odd_behind[:, cols:pack], odd_behind[:, :cols])
    back = back + dot_left(odd_behind[:, pack + cols :], odd_behind[:, pack : pack + cols])
    ham_c = forward[:rows, :cols] + back[:rows]
    ovl_c = forward[rows:, :cols] + back[rows:] + coeff.astype(jnp.float32)
    both_c = jnp.concatenate([ham_c, ovl_c], axis=1)

    dir_f = direction.astype(jnp.float32)
    ham_line = 2.0 * jnp.sum(dir_f * forward[:rows, cols:], axis=0)
    ovl_line = jnp.sum(dir_f * (2.0 * forward[rows:, cols:] + dir_f), axis=0)

    swapped_c = jnp.concatenate([ovl_c, ham_c], axis=1)
    every_c = [swapped_c] + [over_orb(swapped_c, g) for g in range(1, 4)]
    other_c = swapped(both_c, "c")

    partial = dot_left(
        gram_left.astype(jnp.float32), jnp.concatenate([both_c, other_c], axis=0), HIGH
    )
    chip_axes = ("y", "z", "x")
    chips = lax.axis_size(chip_axes)
    parts = lax.all_to_all(
        partial.reshape(chips, 2 * cols // chips, 2 * cols), chip_axes, 0, 0
    )
    strip = jnp.sum(parts, axis=0) * (1.0 / basis_total)
    strip = after(strip, every_c[1], every_c[3])
    half = lax.all_to_all(
        jnp.broadcast_to(strip[None], (chips,) + strip.shape), chip_axes, 0, 0
    ).reshape(2, cols, 2 * cols)
    other_half = swapped(half, "c")
    mixed = jnp.zeros((rows, cols), jnp.float32)
    for near, grams in ((first_core, half), (~first_core, other_half)):
        for k in range(2):
            theirs = jnp.where(near, every_c[k], every_c[2 + k])
            mixed = mixed + plain_dot(theirs[:, :cols], grams[k, :, :cols], HIGH)
            mixed = mixed + plain_dot(theirs[:, cols:], grams[k, :, cols:], HIGH)
    gradient = (4.0 * ham_c - 2.0 * mixed) * local_full.astype(jnp.float32)

    lines = jnp.stack([ham_line, ovl_line, jnp.sum(dir_f * gradient, axis=0)], axis=0)
    lines = lines + swapped(lines, "c")
    copies = jnp.broadcast_to(lines.reshape(1, -1, BLK), (chips, lines.size // BLK, BLK))
    every_line = lax.all_to_all(copies, chip_axes, 0, 0)
    line_terms = jnp.sum(every_line, axis=0).reshape(lines.shape) * (1.0 / math.sqrt(basis_total))
    return (gradient, line_terms)


def solution(mesh):
    fine = Mesh(mesh.devices.reshape(tuple(SIZES.values())), tuple(SIZES))
    placed = (P(BASIS, "orb"), P(BASIS, "orb")) + (P(BASIS, None),) * 5 + (P(BASIS, "orb"),)
    return jax.shard_map(
        on_device,
        mesh=fine,
        in_specs=placed,
        out_specs=(P(BASIS, "orb"), P(None, "orb")),
        check_vma=False,
    )
```

```python
import math

import jax
import jax.numpy as jnp
from jax import lax
from jax.experimental import pallas as pl
from jax.experimental.pallas import tpu as pltpu
from jax.sharding import Mesh, PartitionSpec as P

BLK = 128
BASIS = ("z", "x", "y", "c")
SIZES = {"z": 8, "x": 4, "y": 2, "c": 2, "orb": 4}
HIGH = lax.Precision.HIGH


def shifted(shard, by):
    count = lax.axis_size(BASIS)
    return lax.ppermute(shard, BASIS, [(i, (i + by) % count) for i in range(count)])


def swapped(shard, axis):
    return lax.ppermute(shard, axis, [(0, 1), (1, 0)])


def expand_mask(mask_blocks):
    grown = jnp.repeat(mask_blocks, BLK, axis=0)
    return jnp.repeat(grown, BLK, axis=1)


def plain_dot(left, right, precision=None):
    return jnp.dot(left, right, precision=precision, preferred_element_type=jnp.float32)


def dot_left(left, right, precision=None):
    return lax.dot_general(
        left, right, (((0,), (0,)), ((), ())),
        precision=precision, preferred_element_type=jnp.float32,
    )


def after(shard, *others):
    def nothing(*refs):
        del refs

    return pl.pallas_call(
        nothing,
        out_shape=jax.ShapeDtypeStruct(shard.shape, shard.dtype),
        in_specs=[pl.BlockSpec(memory_space=pl.ANY)] * (1 + len(others)),
        out_specs=pl.BlockSpec(memory_space=pl.ANY),
        input_output_aliases={0: 0},
    )(shard, *others)


def over_orb(shard, g):
    return lax.ppermute(shard, "orb", [(i, i ^ g) for i in range(SIZES["orb"])])


def packed(who, coeff, nearest, behind_2, behind_4, stacked, ahead_2, ahead_4, every_coeff):
    rows, cols = coeff.shape
    pack = cols + nearest.shape[1]
    width = 2 * pack + 6 * cols

    def kernel(who_ref, coeff_ref, near_ref, b2_ref, b4_ref, own_ref, a2_ref, a4_ref, all_ref, out_ref):
        @pl.when(who_ref[0] == 0)
        def _():
            out_ref[:, :cols] = coeff_ref[...]
            out_ref[:, cols:pack] = near_ref[...]
            out_ref[:, pack : 2 * pack] = b2_ref[:, :pack]
            out_ref[:, 2 * pack : 2 * pack + 2 * cols] = a2_ref[...]
            out_ref[:, 2 * pack + 2 * cols : 2 * pack + 4 * cols] = a4_ref[...]

        @pl.when(who_ref[0] != 0)
        def _():
            out_ref[:, :pack] = b2_ref[:, :pack]
            out_ref[:, pack : 2 * pack] = b4_ref[:, :pack]
            out_ref[:, 2 * pack : 2 * pack + 2 * cols] = own_ref[...]
            out_ref[:, 2 * pack + 2 * cols : 2 * pack + 4 * cols] = a2_ref[...]

        for k in range(2):
            start = 2 * pack + (4 + k) * cols
            out_ref[:, start : start + cols] = all_ref[who_ref[1 + k]]

    return pl.pallas_call(
        kernel,
        out_shape=jax.ShapeDtypeStruct((rows, width), coeff.dtype),
        in_specs=[pl.BlockSpec(memory_space=pltpu.SMEM)]
        + [pl.BlockSpec(memory_space=pltpu.VMEM)] * 8,
        out_specs=pl.BlockSpec(memory_space=pltpu.VMEM),
        compiler_params=pltpu.CompilerParams(vmem_limit_bytes=16 * 2**20),
        cost_estimate=pl.CostEstimate(flops=0, bytes_accessed=4 * rows * width, transcendentals=0),
    )(who, coeff, nearest, behind_2, behind_4, stacked, ahead_2, ahead_4, every_coeff)


def on_device(coeffs, direction, ham_diag, ovl_diag, ham_band, ovl_band, band_mask, local_mask):
    rows = coeffs.shape[0]
    cols = coeffs.shape[1]
    basis_total = rows * lax.axis_size(BASIS)
    core = lax.axis_index("c")
    first_core = core == 0
    local_full = expand_mask(local_mask).astype(jnp.bfloat16)
    coeff = coeffs * local_full
    stacked = jnp.concatenate([coeff, direction], axis=1)
    band_full = expand_mask(band_mask).astype(jnp.bfloat16)
    ham_tiles = ham_band * band_full
    ovl_tiles = ovl_band * band_full

    def tile(step):
        part = slice((step - 1) * rows, step * rows)
        return jnp.concatenate([ham_tiles[:, part], ovl_tiles[:, part]], axis=1)

    ahead_2 = shifted(stacked, -2)
    ahead_4 = shifted(stacked, -4)
    spare = jnp.where(first_core, tile(3), tile(1))
    behind_2 = shifted(jnp.concatenate([coeff, spare, tile(2)], axis=1), 2)
    behind_4 = shifted(jnp.concatenate([coeff, tile(3), tile(4)], axis=1), 4)
    place = lax.axis_index("orb")
    every_coeff = lax.all_to_all(
        jnp.broadcast_to(after(coeff, stacked)[None], (SIZES["orb"], rows, cols)), "orb", 0, 0
    )

    def peer(g):
        return lax.dynamic_index_in_dim(every_coeff, place ^ g, 0, keepdims=False)

    near_peers = [peer(2 * core + k) for k in range(2)]
    pack = cols + 2 * rows
    who = jnp.stack([core, place ^ (2 - 2 * core), place ^ (3 - 2 * core)]).astype(jnp.int32)
    crossed = swapped(
        packed(who, coeff, tile(1), behind_2, behind_4, stacked, ahead_2, ahead_4, every_coeff), "c"
    )
    odd_behind = crossed[:, : 2 * pack]
    odd_ahead = crossed[:, 2 * pack : 2 * pack + 4 * cols]
    gram_left = jnp.concatenate(
        [
            jnp.concatenate(near_peers, axis=1),
            crossed[:, 2 * pack + 4 * cols :],
        ],
        axis=0,
    )

    def upright(step):
        part = slice((step - 1) * rows, step * rows)
        return jnp.concatenate([ham_tiles[:, part], ovl_tiles[:, part]], axis=0)

    forward = plain_dot(jnp.concatenate([ham_diag, ovl_diag], axis=0), stacked)
    forward = forward + plain_dot(upright(2), ahead_2)
    forward = forward + plain_dot(upright(4), ahead_4)
    forward = forward + plain_dot(upright(1), odd_ahead[:, : 2 * cols])
    forward = forward + plain_dot(upright(3), odd_ahead[:, 2 * cols :])
    back = dot_left(jnp.concatenate([ham_diag, ovl_diag], axis=1), coeff)
    back = back + dot_left(behind_2[:, pack:], behind_2[:, :cols])
    back = back + dot_left(behind_4[:, pack:], behind_4[:, :cols])
    back = back + dot_left(odd_behind[:, cols:pack], odd_behind[:, :cols])
    back = back + dot_left(odd_behind[:, pack + cols :], odd_behind[:, pack : pack + cols])
    ham_c = forward[:rows, :cols] + back[:rows]
    ovl_c = forward[rows:, :cols] + back[rows:] + coeff.astype(jnp.float32)
    both_c = jnp.concatenate([ham_c, ovl_c], axis=1)

    dir_f = direction.astype(jnp.float32)
    ham_line = 2.0 * jnp.sum(dir_f * forward[:rows, cols:], axis=0)
    ovl_line = jnp.sum(dir_f * (2.0 * forward[rows:, cols:] + dir_f), axis=0)

    swapped_c = jnp.concatenate([ovl_c, ham_c], axis=1)
    every_c = [swapped_c] + [over_orb(swapped_c, g) for g in range(1, 4)]
    other_c = swapped(both_c, "c")

    partial = dot_left(
        gram_left.astype(jnp.float32), jnp.concatenate([both_c, other_c], axis=0), HIGH
    )
    chip_axes = ("y", "z", "x")
    chips = lax.axis_size(chip_axes)
    parts = lax.all_to_all(
        partial.reshape(chips, 2 * cols // chips, 2 * cols), chip_axes, 0, 0
    )
    strip = jnp.sum(parts, axis=0) * (1.0 / basis_total)
    strip = after(strip, every_c[1], every_c[2])
    every_c[2] = after(every_c[2], strip)
    every_c[3] = after(every_c[3], strip)
    half = lax.all_to_all(
        jnp.broadcast_to(strip[None], (chips,) + strip.shape), chip_axes, 0, 0
    ).reshape(2, cols, 2 * cols)
    other_half = swapped(half, "c")
    mixed = jnp.zeros((rows, cols), jnp.float32)
    for near, grams in ((first_core, half), (~first_core, other_half)):
        for k in range(2):
            theirs = jnp.where(near, every_c[k], every_c[2 + k])
            mixed = mixed + plain_dot(theirs[:, :cols], grams[k, :, :cols], HIGH)
            mixed = mixed + plain_dot(theirs[:, cols:], grams[k, :, cols:], HIGH)
    gradient = (4.0 * ham_c - 2.0 * mixed) * local_full.astype(jnp.float32)

    lines = jnp.stack([ham_line, ovl_line, jnp.sum(dir_f * gradient, axis=0)], axis=0)
    lines = lines + swapped(lines, "c")
    copies = jnp.broadcast_to(lines.reshape(1, -1, BLK), (chips, lines.size // BLK, BLK))
    every_line = lax.all_to_all(copies, chip_axes, 0, 0)
    line_terms = jnp.sum(every_line, axis=0).reshape(lines.shape) * (1.0 / math.sqrt(basis_total))
    return (gradient, line_terms)


def solution(mesh):
    fine = Mesh(mesh.devices.reshape(tuple(SIZES.values())), tuple(SIZES))
    placed = (P(BASIS, "orb"), P(BASIS, "orb")) + (P(BASIS, None),) * 5 + (P(BASIS, "orb"),)
    return jax.shard_map(
        on_device,
        mesh=fine,
        in_specs=placed,
        out_specs=(P(BASIS, "orb"), P(None, "orb")),
        check_vma=False,
    )
```

```python
import math

import jax
import jax.numpy as jnp
from jax import lax
from jax.experimental import pallas as pl
from jax.experimental.pallas import tpu as pltpu
from jax.sharding import Mesh, PartitionSpec as P

BLK = 128
BASIS = ("z", "x", "y", "c")
SIZES = {"z": 8, "x": 4, "y": 2, "c": 2, "orb": 4}
HIGH = lax.Precision.HIGH


def shifted(shard, by):
    count = lax.axis_size(BASIS)
    return lax.ppermute(shard, BASIS, [(i, (i + by) % count) for i in range(count)])


def swapped(shard, axis):
    return lax.ppermute(shard, axis, [(0, 1), (1, 0)])


def expand_mask(mask_blocks):
    grown = jnp.repeat(mask_blocks, BLK, axis=0)
    return jnp.repeat(grown, BLK, axis=1)


def plain_dot(left, right, precision=None):
    return jnp.dot(left, right, precision=precision, preferred_element_type=jnp.float32)


def dot_left(left, right, precision=None):
    return lax.dot_general(
        left, right, (((0,), (0,)), ((), ())),
        precision=precision, preferred_element_type=jnp.float32,
    )


def after(shard, *others):
    def nothing(*refs):
        del refs

    return pl.pallas_call(
        nothing,
        out_shape=jax.ShapeDtypeStruct(shard.shape, shard.dtype),
        in_specs=[pl.BlockSpec(memory_space=pl.ANY)] * (1 + len(others)),
        out_specs=pl.BlockSpec(memory_space=pl.ANY),
        input_output_aliases={0: 0},
    )(shard, *others)


def over_orb(shard, by):
    orbs = SIZES["orb"]
    return lax.ppermute(shard, "orb", [(i, (i + by) % orbs) for i in range(orbs)])


def packed(who, coeff, nearest, behind_2, behind_4, stacked, ahead_2, ahead_4, every_coeff):
    rows, cols = coeff.shape
    pack = cols + nearest.shape[1]
    width = 2 * pack + 6 * cols

    def kernel(who_ref, coeff_ref, near_ref, b2_ref, b4_ref, own_ref, a2_ref, a4_ref, all_ref, out_ref):
        @pl.when(who_ref[0] == 0)
        def _():
            out_ref[:, :cols] = coeff_ref[...]
            out_ref[:, cols:pack] = near_ref[...]
            out_ref[:, pack : 2 * pack] = b2_ref[:, :pack]
            out_ref[:, 2 * pack : 2 * pack + 2 * cols] = a2_ref[...]
            out_ref[:, 2 * pack + 2 * cols : 2 * pack + 4 * cols] = a4_ref[...]

        @pl.when(who_ref[0] != 0)
        def _():
            out_ref[:, :pack] = b2_ref[:, :pack]
            out_ref[:, pack : 2 * pack] = b4_ref[:, :pack]
            out_ref[:, 2 * pack : 2 * pack + 2 * cols] = own_ref[...]
            out_ref[:, 2 * pack + 2 * cols : 2 * pack + 4 * cols] = a2_ref[...]

        for k in range(2):
            start = 2 * pack + (4 + k) * cols
            out_ref[:, start : start + cols] = all_ref[who_ref[1 + k]]

    return pl.pallas_call(
        kernel,
        out_shape=jax.ShapeDtypeStruct((rows, width), coeff.dtype),
        in_specs=[pl.BlockSpec(memory_space=pltpu.SMEM)]
        + [pl.BlockSpec(memory_space=pltpu.VMEM)] * 8,
        out_specs=pl.BlockSpec(memory_space=pltpu.VMEM),
        compiler_params=pltpu.CompilerParams(vmem_limit_bytes=16 * 2**20),
        cost_estimate=pl.CostEstimate(flops=0, bytes_accessed=4 * rows * width, transcendentals=0),
    )(who, coeff, nearest, behind_2, behind_4, stacked, ahead_2, ahead_4, every_coeff)


def on_device(coeffs, direction, ham_diag, ovl_diag, ham_band, ovl_band, band_mask, local_mask):
    rows = coeffs.shape[0]
    cols = coeffs.shape[1]
    basis_total = rows * lax.axis_size(BASIS)
    core = lax.axis_index("c")
    first_core = core == 0
    local_full = expand_mask(local_mask).astype(jnp.bfloat16)
    coeff = coeffs * local_full
    stacked = jnp.concatenate([coeff, direction], axis=1)
    band_full = expand_mask(band_mask).astype(jnp.bfloat16)
    ham_tiles = ham_band * band_full
    ovl_tiles = ovl_band * band_full

    def tile(step):
        part = slice((step - 1) * rows, step * rows)
        return jnp.concatenate([ham_tiles[:, part], ovl_tiles[:, part]], axis=1)

    ahead_2 = shifted(stacked, -2)
    ahead_4 = shifted(stacked, -4)
    spare = jnp.where(first_core, tile(3), tile(1))
    sent_2 = jnp.concatenate([coeff, spare, tile(2)], axis=1)
    sent_4 = jnp.concatenate([coeff, tile(3), tile(4)], axis=1)
    behind_2 = shifted(sent_2, 2)
    behind_4 = shifted(sent_4, 4)
    place = lax.axis_index("orb")
    every_coeff = lax.all_gather(after(coeff, stacked, sent_2, sent_4), "orb", axis=0)

    def peer(g):
        return lax.dynamic_index_in_dim(every_coeff, (place + g) % SIZES["orb"], 0, keepdims=False)

    near_peers = [peer(2 * core + k) for k in range(2)]
    pack = cols + 2 * rows
    wanted = [(place + 2 - 2 * core + k) % SIZES["orb"] for k in range(2)]
    who = jnp.stack([core] + wanted).astype(jnp.int32)
    crossed = swapped(
        packed(who, coeff, tile(1), behind_2, behind_4, stacked, ahead_2, ahead_4, every_coeff), "c"
    )
    odd_behind = crossed[:, : 2 * pack]
    odd_ahead = crossed[:, 2 * pack : 2 * pack + 4 * cols]
    gram_left = jnp.concatenate(
        [
            jnp.concatenate(near_peers, axis=1),
            crossed[:, 2 * pack + 4 * cols :],
        ],
        axis=0,
    )

    def upright(step):
        part = slice((step - 1) * rows, step * rows)
        return jnp.concatenate([ham_tiles[:, part], ovl_tiles[:, part]], axis=0)

    forward = plain_dot(jnp.concatenate([ham_diag, ovl_diag], axis=0), stacked)
    forward = forward + plain_dot(upright(2), ahead_2)
    forward = forward + plain_dot(upright(4), ahead_4)
    forward = forward + plain_dot(upright(1), odd_ahead[:, : 2 * cols])
    forward = forward + plain_dot(upright(3), odd_ahead[:, 2 * cols :])
    back = dot_left(jnp.concatenate([ham_diag, ovl_diag], axis=1), coeff)
    back = back + dot_left(behind_2[:, pack:], behind_2[:, :cols])
    back = back + dot_left(behind_4[:, pack:], behind_4[:, :cols])
    back = back + dot_left(odd_behind[:, cols:pack], odd_behind[:, :cols])
    back = back + dot_left(odd_behind[:, pack + cols :], odd_behind[:, pack : pack + cols])
    ham_c = forward[:rows, :cols] + back[:rows]
    ovl_c = forward[rows:, :cols] + back[rows:] + coeff.astype(jnp.float32)
    both_c = jnp.concatenate([ham_c, ovl_c], axis=1)

    dir_f = direction.astype(jnp.float32)
    ham_line = 2.0 * jnp.sum(dir_f * forward[:rows, cols:], axis=0)
    ovl_line = jnp.sum(dir_f * (2.0 * forward[rows:, cols:] + dir_f), axis=0)

    swapped_c = jnp.concatenate([ovl_c, ham_c], axis=1)
    next_c, last_c = over_orb(swapped_c, -1), over_orb(swapped_c, 1)
    other_c = swapped(both_c, "c")

    partial = dot_left(
        gram_left.astype(jnp.float32), jnp.concatenate([both_c, other_c], axis=0), HIGH
    )
    chip_axes = ("y", "z", "x")
    chips = lax.axis_size(chip_axes)
    parts = lax.all_to_all(
        partial.reshape(chips, 2 * cols // chips, 2 * cols), chip_axes, 0, 0
    )
    strip = jnp.sum(parts, axis=0) * (1.0 / basis_total)
    strip = after(strip, next_c, last_c)
    top = over_orb(after(next_c[: rows // 2], strip), -1)
    bottom = over_orb(after(last_c[rows // 2 :], strip), 1)
    every_c = [swapped_c, next_c, jnp.concatenate([top, bottom], axis=0), last_c]
    half = lax.all_to_all(
        jnp.broadcast_to(strip[None], (chips,) + strip.shape), chip_axes, 0, 0
    ).reshape(2, cols, 2 * cols)
    other_half = swapped(half, "c")
    mixed = jnp.zeros((rows, cols), jnp.float32)
    for near, grams in ((first_core, half), (~first_core, other_half)):
        for k in range(2):
            theirs = jnp.where(near, every_c[k], every_c[2 + k])
            mixed = mixed + plain_dot(theirs[:, :cols], grams[k, :, :cols], HIGH)
            mixed = mixed + plain_dot(theirs[:, cols:], grams[k, :, cols:], HIGH)
    gradient = (4.0 * ham_c - 2.0 * mixed) * local_full.astype(jnp.float32)

    lines = jnp.stack([ham_line, ovl_line, jnp.sum(dir_f * gradient, axis=0)], axis=0)
    lines = lines + swapped(lines, "c")
    copies = jnp.broadcast_to(lines.reshape(1, -1, BLK), (chips, lines.size // BLK, BLK))
    every_line = lax.all_to_all(copies, chip_axes, 0, 0)
    line_terms = jnp.sum(every_line, axis=0).reshape(lines.shape) * (1.0 / math.sqrt(basis_total))
    return (gradient, line_terms)


def solution(mesh):
    fine = Mesh(mesh.devices.reshape(tuple(SIZES.values())), tuple(SIZES))
    placed = (P(BASIS, "orb"), P(BASIS, "orb")) + (P(BASIS, None),) * 5 + (P(BASIS, "orb"),)
    return jax.shard_map(
        on_device,
        mesh=fine,
        in_specs=placed,
        out_specs=(P(BASIS, "orb"), P(None, "orb")),
        check_vma=False,
    )
```

```python
import math

import jax
import jax.numpy as jnp
from jax import lax
from jax.experimental import pallas as pl
from jax.experimental.pallas import tpu as pltpu
from jax.sharding import Mesh, PartitionSpec as P

BLK = 128
BASIS = ("z", "x", "y", "c")
SIZES = {"z": 8, "x": 4, "y": 2, "c": 2, "orb": 4}
HIGH = lax.Precision.HIGH


def shifted(shard, by):
    count = lax.axis_size(BASIS)
    return lax.ppermute(shard, BASIS, [(i, (i + by) % count) for i in range(count)])


def swapped(shard, axis):
    return lax.ppermute(shard, axis, [(0, 1), (1, 0)])


def expand_mask(mask_blocks):
    grown = jnp.repeat(mask_blocks, BLK, axis=0)
    return jnp.repeat(grown, BLK, axis=1)


def plain_dot(left, right, precision=None):
    return jnp.dot(left, right, precision=precision, preferred_element_type=jnp.float32)


def dot_left(left, right, precision=None):
    return lax.dot_general(
        left, right, (((0,), (0,)), ((), ())),
        precision=precision, preferred_element_type=jnp.float32,
    )


def after(shard, *others):
    def nothing(*refs):
        del refs

    return pl.pallas_call(
        nothing,
        out_shape=jax.ShapeDtypeStruct(shard.shape, shard.dtype),
        in_specs=[pl.BlockSpec(memory_space=pl.ANY)] * (1 + len(others)),
        out_specs=pl.BlockSpec(memory_space=pl.ANY),
        input_output_aliases={0: 0},
    )(shard, *others)


def over_orb(shard, by):
    orbs = SIZES["orb"]
    return lax.ppermute(shard, "orb", [(i, (i + by) % orbs) for i in range(orbs)])


def packed(who, coeff, nearest, behind_2, behind_4, stacked, ahead_2, ahead_4, every_coeff):
    rows, cols = coeff.shape
    pack = cols + nearest.shape[1]
    width = 2 * pack + 6 * cols

    def kernel(who_ref, coeff_ref, near_ref, b2_ref, b4_ref, own_ref, a2_ref, a4_ref, all_ref, out_ref):
        @pl.when(who_ref[0] == 0)
        def _():
            out_ref[:, :cols] = coeff_ref[...]
            out_ref[:, cols:pack] = near_ref[...]
            out_ref[:, pack : 2 * pack] = b2_ref[:, :pack]
            out_ref[:, 2 * pack : 2 * pack + 2 * cols] = a2_ref[...]
            out_ref[:, 2 * pack + 2 * cols : 2 * pack + 4 * cols] = a4_ref[...]

        @pl.when(who_ref[0] != 0)
        def _():
            out_ref[:, :pack] = b2_ref[:, :pack]
            out_ref[:, pack : 2 * pack] = b4_ref[:, :pack]
            out_ref[:, 2 * pack : 2 * pack + 2 * cols] = own_ref[...]
            out_ref[:, 2 * pack + 2 * cols : 2 * pack + 4 * cols] = a2_ref[...]

        for k in range(2):
            start = 2 * pack + (4 + k) * cols
            out_ref[:, start : start + cols] = all_ref[who_ref[1 + k]]

    return pl.pallas_call(
        kernel,
        out_shape=jax.ShapeDtypeStruct((rows, width), coeff.dtype),
        in_specs=[pl.BlockSpec(memory_space=pltpu.SMEM)]
        + [pl.BlockSpec(memory_space=pltpu.VMEM)] * 8,
        out_specs=pl.BlockSpec(memory_space=pltpu.VMEM),
        compiler_params=pltpu.CompilerParams(vmem_limit_bytes=16 * 2**20),
        cost_estimate=pl.CostEstimate(flops=0, bytes_accessed=4 * rows * width, transcendentals=0),
    )(who, coeff, nearest, behind_2, behind_4, stacked, ahead_2, ahead_4, every_coeff)


def prepared(who, coeffs, direction, ham_band, ovl_band, band_mask, local_mask):
    rows, cols = coeffs.shape
    reach = ham_band.shape[1] // rows
    pack = cols + 2 * rows

    def kernel(who_ref, c_ref, d_ref, h_ref, s_ref, band_ref, local_ref,
               coeff_ref, stacked_ref, two_ref, four_ref, near_ref, up_ref):
        for i in range(rows // BLK):
            at = slice(i * BLK, (i + 1) * BLK)
            for j in range(cols // BLK):
                block = c_ref[at, j * BLK : (j + 1) * BLK]
                block = jnp.where(local_ref[i, j] != 0, block, jnp.zeros_like(block))
                for ref in (coeff_ref, stacked_ref, two_ref, four_ref):
                    ref[at, j * BLK : (j + 1) * BLK] = block
            stacked_ref[at, cols:] = d_ref[at, :]
            for j in range(reach * rows // BLK):
                step, within = divmod(j * BLK, rows)
                for m, ref in enumerate((h_ref, s_ref)):
                    block = ref[at, j * BLK : (j + 1) * BLK]
                    block = jnp.where(band_ref[i, j] != 0, block, jnp.zeros_like(block))
                    up_ref[step, m * rows + i * BLK : m * rows + (i + 1) * BLK, within : within + BLK] = block
                    start = cols + m * rows + within
                    if step == 0:
                        near_ref[at, start - cols : start - cols + BLK] = block

                        @pl.when(who_ref[0] != 0)
                        def _(block=block, start=start, at=at):
                            two_ref[at, start : start + BLK] = block

                    if step == 1:
                        two_ref[at, start + pack - cols : start + pack - cols + BLK] = block
                    if step == 2:
                        four_ref[at, start : start + BLK] = block

                        @pl.when(who_ref[0] == 0)
                        def _(block=block, start=start, at=at):
                            two_ref[at, start : start + BLK] = block

                    if step == 3:
                        four_ref[at, start + pack - cols : start + pack - cols + BLK] = block

    def like(*shape):
        return jax.ShapeDtypeStruct(shape, coeffs.dtype)

    smem, vmem = pl.BlockSpec(memory_space=pltpu.SMEM), pl.BlockSpec(memory_space=pltpu.VMEM)
    wide = pack + 2 * rows
    return pl.pallas_call(
        kernel,
        out_shape=(
            like(rows, cols), like(rows, 2 * cols), like(rows, wide), like(rows, wide),
            like(rows, 2 * rows), like(reach, 2 * rows, rows),
        ),
        in_specs=[smem] + [vmem] * 4 + [smem] * 2,
        out_specs=(vmem,) * 6,
        compiler_params=pltpu.CompilerParams(vmem_limit_bytes=16 * 2**20),
        cost_estimate=pl.CostEstimate(flops=0, bytes_accessed=20 * rows * wide, transcendentals=0),
    )(who, coeffs, direction, ham_band, ovl_band, band_mask, local_mask)


def summed_copies(parts, scale, *others):
    def kernel(parts_ref, *refs):
        total = parts_ref[0]
        for i in range(1, parts.shape[0]):
            total = total + parts_ref[i]
        total = total * scale
        for i in range(parts.shape[0]):
            refs[-1][i] = total

    return pl.pallas_call(
        kernel,
        out_shape=jax.ShapeDtypeStruct(parts.shape, parts.dtype),
        in_specs=[pl.BlockSpec(memory_space=pltpu.VMEM)]
        + [pl.BlockSpec(memory_space=pl.ANY)] * len(others),
        out_specs=pl.BlockSpec(memory_space=pltpu.VMEM),
        compiler_params=pltpu.CompilerParams(vmem_limit_bytes=16 * 2**20),
        cost_estimate=pl.CostEstimate(flops=parts.size, bytes_accessed=8 * parts.size, transcendentals=0),
    )(parts, *others)


def on_device(coeffs, direction, ham_diag, ovl_diag, ham_band, ovl_band, band_mask, local_mask):
    rows = coeffs.shape[0]
    cols = coeffs.shape[1]
    basis_total = rows * lax.axis_size(BASIS)
    core = lax.axis_index("c")
    first_core = core == 0
    local_full = expand_mask(local_mask).astype(jnp.bfloat16)
    coeff, stacked, sent_2, sent_4, nearest, upright = prepared(
        jnp.stack([core]).astype(jnp.int32),
        coeffs, direction, ham_band, ovl_band, band_mask, local_mask,
    )

    ahead_2 = shifted(stacked, -2)
    ahead_4 = shifted(stacked, -4)
    behind_2 = shifted(sent_2, 2)
    behind_4 = shifted(sent_4, 4)
    place = lax.axis_index("orb")
    every_coeff = lax.all_gather(after(coeff, stacked, sent_2, sent_4), "orb", axis=0)

    def peer(g):
        return lax.dynamic_index_in_dim(every_coeff, (place + g) % SIZES["orb"], 0, keepdims=False)

    near_peers = [peer(2 * core + k) for k in range(2)]
    pack = cols + 2 * rows
    wanted = [(place + 2 - 2 * core + k) % SIZES["orb"] for k in range(2)]
    who = jnp.stack([core] + wanted).astype(jnp.int32)
    crossed = swapped(
        packed(who, coeff, nearest, behind_2, behind_4, stacked, ahead_2, ahead_4, every_coeff), "c"
    )
    odd_behind = crossed[:, : 2 * pack]
    odd_ahead = crossed[:, 2 * pack : 2 * pack + 4 * cols]
    gram_left = jnp.concatenate(
        [
            jnp.concatenate(near_peers, axis=1),
            crossed[:, 2 * pack + 4 * cols :],
        ],
        axis=0,
    )

    forward = plain_dot(jnp.concatenate([ham_diag, ovl_diag], axis=0), stacked)
    forward = forward + plain_dot(upright[1], ahead_2)
    forward = forward + plain_dot(upright[3], ahead_4)
    forward = forward + plain_dot(upright[0], odd_ahead[:, : 2 * cols])
    forward = forward + plain_dot(upright[2], odd_ahead[:, 2 * cols :])
    back = dot_left(jnp.concatenate([ham_diag, ovl_diag], axis=1), coeff)
    back = back + dot_left(behind_2[:, pack:], behind_2[:, :cols])
    back = back + dot_left(behind_4[:, pack:], behind_4[:, :cols])
    back = back + dot_left(odd_behind[:, cols:pack], odd_behind[:, :cols])
    back = back + dot_left(odd_behind[:, pack + cols :], odd_behind[:, pack : pack + cols])
    ham_c = forward[:rows, :cols] + back[:rows]
    ovl_c = forward[rows:, :cols] + back[rows:] + coeff.astype(jnp.float32)
    both_c = jnp.concatenate([ham_c, ovl_c], axis=1)

    dir_f = direction.astype(jnp.float32)
    ham_line = 2.0 * jnp.sum(dir_f * forward[:rows, cols:], axis=0)
    ovl_line = jnp.sum(dir_f * (2.0 * forward[rows:, cols:] + dir_f), axis=0)

    swapped_c = jnp.concatenate([ovl_c, ham_c], axis=1)
    next_c, last_c = over_orb(swapped_c, -1), over_orb(swapped_c, 1)
    other_c = swapped(both_c, "c")

    partial = dot_left(
        gram_left.astype(jnp.float32), jnp.concatenate([both_c, other_c], axis=0), HIGH
    )
    chip_axes = ("y", "z", "x")
    chips = lax.axis_size(chip_axes)
    parts = lax.all_to_all(
        partial.reshape(chips, 2 * cols // chips, 2 * cols), chip_axes, 0, 0
    )
    copies = summed_copies(
        parts, 1.0 / basis_total, next_c[:8, :BLK], last_c[:8, :BLK]
    )
    top = over_orb(after(next_c[: rows // 2], copies), -1)
    bottom = over_orb(after(last_c[rows // 2 :], copies), 1)
    every_c = [swapped_c, next_c, jnp.concatenate([top, bottom], axis=0), last_c]
    half = lax.all_to_all(copies, chip_axes, 0, 0).reshape(2, cols, 2 * cols)
    other_half = swapped(half, "c")
    mixed = jnp.zeros((rows, cols), jnp.float32)
    for near, grams in ((first_core, half), (~first_core, other_half)):
        for k in range(2):
            theirs = jnp.where(near, every_c[k], every_c[2 + k])
            mixed = mixed + plain_dot(theirs[:, :cols], grams[k, :, :cols], HIGH)
            mixed = mixed + plain_dot(theirs[:, cols:], grams[k, :, cols:], HIGH)
    gradient = (4.0 * ham_c - 2.0 * mixed) * local_full.astype(jnp.float32)

    lines = jnp.stack([ham_line, ovl_line, jnp.sum(dir_f * gradient, axis=0)], axis=0)
    lines = lines + swapped(lines, "c")
    copies = jnp.broadcast_to(lines.reshape(1, -1, BLK), (chips, lines.size // BLK, BLK))
    every_line = lax.all_to_all(copies, chip_axes, 0, 0)
    line_terms = jnp.sum(every_line, axis=0).reshape(lines.shape) * (1.0 / math.sqrt(basis_total))
    return (gradient, line_terms)


def solution(mesh):
    fine = Mesh(mesh.devices.reshape(tuple(SIZES.values())), tuple(SIZES))
    placed = (P(BASIS, "orb"), P(BASIS, "orb")) + (P(BASIS, None),) * 5 + (P(BASIS, "orb"),)
    return jax.shard_map(
        on_device,
        mesh=fine,
        in_specs=placed,
        out_specs=(P(BASIS, "orb"), P(None, "orb")),
        check_vma=False,
    )
```

```python
import math

import jax
import jax.numpy as jnp
from jax import lax
from jax.experimental import pallas as pl
from jax.experimental.pallas import tpu as pltpu
from jax.sharding import Mesh, PartitionSpec as P

BLK = 128
BASIS = ("z", "x", "y", "c")
SIZES = {"z": 8, "x": 4, "y": 2, "c": 2, "orb": 4}
HIGH = lax.Precision.HIGH


def shifted(shard, by):
    count = lax.axis_size(BASIS)
    return lax.ppermute(shard, BASIS, [(i, (i + by) % count) for i in range(count)])


def swapped(shard, axis):
    return lax.ppermute(shard, axis, [(0, 1), (1, 0)])


def expand_mask(mask_blocks):
    grown = jnp.repeat(mask_blocks, BLK, axis=0)
    return jnp.repeat(grown, BLK, axis=1)


def plain_dot(left, right, precision=None):
    return jnp.dot(left, right, precision=precision, preferred_element_type=jnp.float32)


def dot_left(left, right, precision=None):
    return lax.dot_general(
        left, right, (((0,), (0,)), ((), ())),
        precision=precision, preferred_element_type=jnp.float32,
    )


def after(shard, *others):
    def nothing(*refs):
        del refs

    return pl.pallas_call(
        nothing,
        out_shape=jax.ShapeDtypeStruct(shard.shape, shard.dtype),
        in_specs=[pl.BlockSpec(memory_space=pl.ANY)] * (1 + len(others)),
        out_specs=pl.BlockSpec(memory_space=pl.ANY),
        input_output_aliases={0: 0},
    )(shard, *others)


def over_orb(shard, by):
    orbs = SIZES["orb"]
    return lax.ppermute(shard, "orb", [(i, (i + by) % orbs) for i in range(orbs)])


def packed(who, coeff, nearest, behind_2, behind_4, stacked, ahead_2, ahead_4, every_coeff):
    rows, cols = coeff.shape
    pack = cols + nearest.shape[1]
    width = 2 * pack + 6 * cols

    def kernel(who_ref, coeff_ref, near_ref, b2_ref, b4_ref, own_ref, a2_ref, a4_ref, all_ref, out_ref):
        @pl.when(who_ref[0] == 0)
        def _():
            out_ref[:, :cols] = coeff_ref[...]
            out_ref[:, cols:pack] = near_ref[...]
            out_ref[:, pack : 2 * pack] = b2_ref[:, :pack]
            out_ref[:, 2 * pack : 2 * pack + 2 * cols] = a2_ref[...]
            out_ref[:, 2 * pack + 2 * cols : 2 * pack + 4 * cols] = a4_ref[...]

        @pl.when(who_ref[0] != 0)
        def _():
            out_ref[:, :pack] = b2_ref[:, :pack]
            out_ref[:, pack : 2 * pack] = b4_ref[:, :pack]
            out_ref[:, 2 * pack : 2 * pack + 2 * cols] = own_ref[...]
            out_ref[:, 2 * pack + 2 * cols : 2 * pack + 4 * cols] = a2_ref[...]

        for k in range(2):
            start = 2 * pack + (4 + k) * cols
            out_ref[:, start : start + cols] = all_ref[who_ref[1 + k]]

    return pl.pallas_call(
        kernel,
        out_shape=jax.ShapeDtypeStruct((rows, width), coeff.dtype),
        in_specs=[pl.BlockSpec(memory_space=pltpu.SMEM)]
        + [pl.BlockSpec(memory_space=pltpu.VMEM)] * 8,
        out_specs=pl.BlockSpec(memory_space=pltpu.VMEM),
        compiler_params=pltpu.CompilerParams(vmem_limit_bytes=16 * 2**20),
        cost_estimate=pl.CostEstimate(flops=0, bytes_accessed=4 * rows * width, transcendentals=0),
    )(who, coeff, nearest, behind_2, behind_4, stacked, ahead_2, ahead_4, every_coeff)


def prepared(who, coeffs, direction, ham_band, ovl_band, band_mask, local_mask):
    rows, cols = coeffs.shape
    reach = ham_band.shape[1] // rows
    pack = cols + 2 * rows

    def kernel(who_ref, *refs):
        sources, outs, held, sems = refs[:6], refs[6:11], refs[11:17], refs[17]
        fetched = [
            pltpu.make_async_copy(source, slot, sems.at[i])
            for i, (source, slot) in enumerate(zip(sources, held))
        ]
        for copy in fetched:
            copy.start()
        for copy in fetched:
            copy.wait()
        c_ref, d_ref, h_ref, s_ref, band_ref, local_ref = held
        coeff_ref, stacked_ref, two_ref, four_ref, near_ref = outs
        for i in range(rows // BLK):
            at = slice(i * BLK, (i + 1) * BLK)
            for j in range(cols // BLK):
                block = c_ref[at, j * BLK : (j + 1) * BLK]
                block = jnp.where(local_ref[i, j] != 0, block, jnp.zeros_like(block))
                for ref in (coeff_ref, stacked_ref, two_ref, four_ref):
                    ref[at, j * BLK : (j + 1) * BLK] = block
            stacked_ref[at, cols:] = d_ref[at, :]
            for j in range(reach * rows // BLK):
                step, within = divmod(j * BLK, rows)
                for m, ref in enumerate((h_ref, s_ref)):
                    block = ref[at, j * BLK : (j + 1) * BLK]
                    block = jnp.where(band_ref[i, j] != 0, block, jnp.zeros_like(block))
                    start = cols + m * rows + within
                    if step == 0:
                        near_ref[at, start - cols : start - cols + BLK] = block

                        @pl.when(who_ref[0] != 0)
                        def _(block=block, start=start, at=at):
                            two_ref[at, start : start + BLK] = block

                    if step == 1:
                        two_ref[at, start + pack - cols : start + pack - cols + BLK] = block
                    if step == 2:
                        four_ref[at, start : start + BLK] = block

                        @pl.when(who_ref[0] == 0)
                        def _(block=block, start=start, at=at):
                            two_ref[at, start : start + BLK] = block

                    if step == 3:
                        four_ref[at, start + pack - cols : start + pack - cols + BLK] = block

    def like(*shape):
        return jax.ShapeDtypeStruct(shape, coeffs.dtype)

    sources = (coeffs, direction, ham_band, ovl_band, band_mask, local_mask)
    vmem = pl.BlockSpec(memory_space=pltpu.VMEM)
    wide = pack + 2 * rows
    return pl.pallas_call(
        kernel,
        out_shape=(
            like(rows, cols), like(rows, 2 * cols), like(rows, wide), like(rows, wide), like(rows, 2 * rows),
        ),
        in_specs=[pl.BlockSpec(memory_space=pltpu.SMEM)]
        + [pl.BlockSpec(memory_space=pltpu.HBM)] * len(sources),
        out_specs=(vmem,) * 5,
        scratch_shapes=[pltpu.VMEM(source.shape, source.dtype) for source in sources[:4]]
        + [pltpu.SMEM(source.shape, source.dtype) for source in sources[4:]]
        + [pltpu.SemaphoreType.DMA((len(sources),))],
        compiler_params=pltpu.CompilerParams(vmem_limit_bytes=60 * 2**20),
        cost_estimate=pl.CostEstimate(flops=0, bytes_accessed=20 * rows * wide, transcendentals=0),
    )(who, *sources)


def summed_copies(parts, scale, *others):
    def kernel(parts_ref, *refs):
        total = parts_ref[0]
        for i in range(1, parts.shape[0]):
            total = total + parts_ref[i]
        total = total * scale
        for i in range(parts.shape[0]):
            refs[-1][i] = total

    return pl.pallas_call(
        kernel,
        out_shape=jax.ShapeDtypeStruct(parts.shape, parts.dtype),
        in_specs=[pl.BlockSpec(memory_space=pltpu.VMEM)]
        + [pl.BlockSpec(memory_space=pl.ANY)] * len(others),
        out_specs=pl.BlockSpec(memory_space=pltpu.VMEM),
        compiler_params=pltpu.CompilerParams(vmem_limit_bytes=16 * 2**20),
        cost_estimate=pl.CostEstimate(flops=parts.size, bytes_accessed=8 * parts.size, transcendentals=0),
    )(parts, *others)


def on_device(coeffs, direction, ham_diag, ovl_diag, ham_band, ovl_band, band_mask, local_mask):
    rows = coeffs.shape[0]
    cols = coeffs.shape[1]
    basis_total = rows * lax.axis_size(BASIS)
    core = lax.axis_index("c")
    first_core = core == 0
    local_full = expand_mask(local_mask).astype(jnp.bfloat16)
    coeff, stacked, sent_2, sent_4, nearest = prepared(
        jnp.stack([core]).astype(jnp.int32),
        coeffs, direction, ham_band, ovl_band, band_mask, local_mask,
    )

    ahead_2 = shifted(stacked, -2)
    ahead_4 = shifted(stacked, -4)
    behind_2 = shifted(sent_2, 2)
    behind_4 = shifted(sent_4, 4)
    place = lax.axis_index("orb")
    every_coeff = lax.all_gather(after(coeff, stacked, sent_2, sent_4), "orb", axis=0)

    def peer(g):
        return lax.dynamic_index_in_dim(every_coeff, (place + g) % SIZES["orb"], 0, keepdims=False)

    near_peers = [peer(2 * core + k) for k in range(2)]
    pack = cols + 2 * rows
    wanted = [(place + 2 - 2 * core + k) % SIZES["orb"] for k in range(2)]
    who = jnp.stack([core] + wanted).astype(jnp.int32)
    crossed = swapped(
        packed(who, coeff, nearest, behind_2, behind_4, stacked, ahead_2, ahead_4, every_coeff), "c"
    )
    odd_behind = crossed[:, : 2 * pack]
    odd_ahead = crossed[:, 2 * pack : 2 * pack + 4 * cols]
    gram_left = jnp.concatenate(
        [
            jnp.concatenate(near_peers, axis=1),
            crossed[:, 2 * pack + 4 * cols :],
        ],
        axis=0,
    )

    band_full = expand_mask(band_mask).astype(jnp.bfloat16)
    upright = [
        jnp.concatenate(
            [(band * band_full)[:, k * rows : (k + 1) * rows] for band in (ham_band, ovl_band)], axis=0
        )
        for k in range(ham_band.shape[1] // rows)
    ]

    forward = plain_dot(jnp.concatenate([ham_diag, ovl_diag], axis=0), stacked)
    forward = forward + plain_dot(upright[1], ahead_2)
    forward = forward + plain_dot(upright[3], ahead_4)
    forward = forward + plain_dot(upright[0], odd_ahead[:, : 2 * cols])
    forward = forward + plain_dot(upright[2], odd_ahead[:, 2 * cols :])
    back = dot_left(jnp.concatenate([ham_diag, ovl_diag], axis=1), coeff)
    back = back + dot_left(behind_2[:, pack:], behind_2[:, :cols])
    back = back + dot_left(behind_4[:, pack:], behind_4[:, :cols])
    back = back + dot_left(odd_behind[:, cols:pack], odd_behind[:, :cols])
    back = back + dot_left(odd_behind[:, pack + cols :], odd_behind[:, pack : pack + cols])
    ham_c = forward[:rows, :cols] + back[:rows]
    ovl_c = forward[rows:, :cols] + back[rows:] + coeff.astype(jnp.float32)
    both_c = jnp.concatenate([ham_c, ovl_c], axis=1)

    dir_f = direction.astype(jnp.float32)
    ham_line = 2.0 * jnp.sum(dir_f * forward[:rows, cols:], axis=0)
    ovl_line = jnp.sum(dir_f * (2.0 * forward[rows:, cols:] + dir_f), axis=0)

    swapped_c = jnp.concatenate([ovl_c, ham_c], axis=1)
    next_c, last_c = over_orb(swapped_c, -1), over_orb(swapped_c, 1)
    other_c = swapped(both_c, "c")

    partial = dot_left(
        gram_left.astype(jnp.float32), jnp.concatenate([both_c, other_c], axis=0), HIGH
    )
    chip_axes = ("y", "z", "x")
    chips = lax.axis_size(chip_axes)
    parts = lax.all_to_all(
        partial.reshape(chips, 2 * cols // chips, 2 * cols), chip_axes, 0, 0
    )
    copies = summed_copies(
        parts, 1.0 / basis_total, next_c[:8, :BLK], last_c[:8, :BLK]
    )
    top = over_orb(after(next_c[: rows // 2], copies), -1)
    bottom = over_orb(after(last_c[rows // 2 :], copies), 1)
    every_c = [swapped_c, next_c, jnp.concatenate([top, bottom], axis=0), last_c]
    half = lax.all_to_all(copies, chip_axes, 0, 0).reshape(2, cols, 2 * cols)
    other_half = swapped(half, "c")
    mixed = jnp.zeros((rows, cols), jnp.float32)
    for near, grams in ((first_core, half), (~first_core, other_half)):
        for k in range(2):
            theirs = jnp.where(near, every_c[k], every_c[2 + k])
            mixed = mixed + plain_dot(theirs[:, :cols], grams[k, :, :cols], HIGH)
            mixed = mixed + plain_dot(theirs[:, cols:], grams[k, :, cols:], HIGH)
    gradient = (4.0 * ham_c - 2.0 * mixed) * local_full.astype(jnp.float32)

    lines = jnp.stack([ham_line, ovl_line, jnp.sum(dir_f * gradient, axis=0)], axis=0)
    lines = lines + swapped(lines, "c")
    copies = jnp.broadcast_to(lines.reshape(1, -1, BLK), (chips, lines.size // BLK, BLK))
    every_line = lax.all_to_all(copies, chip_axes, 0, 0)
    line_terms = jnp.sum(every_line, axis=0).reshape(lines.shape) * (1.0 / math.sqrt(basis_total))
    return (gradient, line_terms)


def solution(mesh):
    fine = Mesh(mesh.devices.reshape(tuple(SIZES.values())), tuple(SIZES))
    placed = (P(BASIS, "orb"), P(BASIS, "orb")) + (P(BASIS, None),) * 5 + (P(BASIS, "orb"),)
    return jax.shard_map(
        on_device,
        mesh=fine,
        in_specs=placed,
        out_specs=(P(BASIS, "orb"), P(None, "orb")),
        check_vma=False,
    )
```

```python
import math

import jax
import jax.numpy as jnp
from jax import lax
from jax.experimental import pallas as pl
from jax.experimental.pallas import tpu as pltpu
from jax.sharding import Mesh, PartitionSpec as P

BLK = 128
BASIS = ("z", "x", "y", "c")
SIZES = {"z": 8, "x": 4, "y": 2, "c": 2, "orb": 4}
HIGH = lax.Precision.HIGH


def shifted(shard, by):
    count = lax.axis_size(BASIS)
    return lax.ppermute(shard, BASIS, [(i, (i + by) % count) for i in range(count)])


def swapped(shard, axis):
    return lax.ppermute(shard, axis, [(0, 1), (1, 0)])


def expand_mask(mask_blocks):
    grown = jnp.repeat(mask_blocks, BLK, axis=0)
    return jnp.repeat(grown, BLK, axis=1)


def plain_dot(left, right, precision=None):
    return jnp.dot(left, right, precision=precision, preferred_element_type=jnp.float32)


def dot_left(left, right, precision=None):
    return lax.dot_general(
        left, right, (((0,), (0,)), ((), ())),
        precision=precision, preferred_element_type=jnp.float32,
    )


def after(shard, *others):
    def nothing(*refs):
        del refs

    return pl.pallas_call(
        nothing,
        out_shape=jax.ShapeDtypeStruct(shard.shape, shard.dtype),
        in_specs=[pl.BlockSpec(memory_space=pl.ANY)] * (1 + len(others)),
        out_specs=pl.BlockSpec(memory_space=pl.ANY),
        input_output_aliases={0: 0},
    )(shard, *others)


def over_orb(shard, by):
    orbs = SIZES["orb"]
    return lax.ppermute(shard, "orb", [(i, (i + by) % orbs) for i in range(orbs)])


def packed(who, coeff, nearest, behind_2, behind_4, stacked, ahead_2, ahead_4, every_coeff):
    rows, cols = coeff.shape
    pack = cols + nearest.shape[1]
    width = 2 * pack + 6 * cols

    def kernel(who_ref, coeff_ref, near_ref, b2_ref, b4_ref, own_ref, a2_ref, a4_ref, all_ref, out_ref):
        @pl.when(who_ref[0] == 0)
        def _():
            out_ref[:, :cols] = coeff_ref[...]
            out_ref[:, cols:pack] = near_ref[...]
            out_ref[:, pack : 2 * pack] = b2_ref[:, :pack]
            out_ref[:, 2 * pack : 2 * pack + 2 * cols] = a2_ref[...]
            out_ref[:, 2 * pack + 2 * cols : 2 * pack + 4 * cols] = a4_ref[...]

        @pl.when(who_ref[0] != 0)
        def _():
            out_ref[:, :pack] = b2_ref[:, :pack]
            out_ref[:, pack : 2 * pack] = b4_ref[:, :pack]
            out_ref[:, 2 * pack : 2 * pack + 2 * cols] = own_ref[...]
            out_ref[:, 2 * pack + 2 * cols : 2 * pack + 4 * cols] = a2_ref[...]

        for k in range(2):
            start = 2 * pack + (4 + k) * cols
            out_ref[:, start : start + cols] = all_ref[who_ref[1 + k]]

    return pl.pallas_call(
        kernel,
        out_shape=jax.ShapeDtypeStruct((rows, width), coeff.dtype),
        in_specs=[pl.BlockSpec(memory_space=pltpu.SMEM)]
        + [pl.BlockSpec(memory_space=pltpu.VMEM)] * 8,
        out_specs=pl.BlockSpec(memory_space=pltpu.VMEM),
        compiler_params=pltpu.CompilerParams(vmem_limit_bytes=16 * 2**20),
        cost_estimate=pl.CostEstimate(flops=0, bytes_accessed=4 * rows * width, transcendentals=0),
    )(who, coeff, nearest, behind_2, behind_4, stacked, ahead_2, ahead_4, every_coeff)


def prepared(who, coeffs, direction, ham_band, ovl_band, band_mask, local_mask):
    rows, cols = coeffs.shape
    reach = ham_band.shape[1] // rows
    pack = cols + 2 * rows

    def kernel(who_ref, *refs):
        sources, outs, held, sems = refs[:6], refs[6:11], refs[11:17], refs[17]
        fetched = [
            pltpu.make_async_copy(source, slot, sems.at[i])
            for i, (source, slot) in enumerate(zip(sources, held))
        ]
        for copy in fetched:
            copy.start()
        for copy in fetched:
            copy.wait()
        c_ref, d_ref, h_ref, s_ref, band_ref, local_ref = held
        coeff_ref, stacked_ref, two_ref, four_ref, near_ref = outs
        for i in range(rows // BLK):
            at = slice(i * BLK, (i + 1) * BLK)
            for j in range(cols // BLK):
                block = c_ref[at, j * BLK : (j + 1) * BLK]
                block = jnp.where(local_ref[i, j] != 0, block, jnp.zeros_like(block))
                for ref in (coeff_ref, stacked_ref, two_ref, four_ref):
                    ref[at, j * BLK : (j + 1) * BLK] = block
            stacked_ref[at, cols:] = d_ref[at, :]
            for j in range(reach * rows // BLK):
                step, within = divmod(j * BLK, rows)
                for m, ref in enumerate((h_ref, s_ref)):
                    block = ref[at, j * BLK : (j + 1) * BLK]
                    block = jnp.where(band_ref[i, j] != 0, block, jnp.zeros_like(block))
                    start = cols + m * rows + within
                    if step == 0:
                        near_ref[at, start - cols : start - cols + BLK] = block

                        @pl.when(who_ref[0] != 0)
                        def _(block=block, start=start, at=at):
                            two_ref[at, start : start + BLK] = block

                    if step == 1:
                        two_ref[at, start + pack - cols : start + pack - cols + BLK] = block
                    if step == 2:
                        four_ref[at, start : start + BLK] = block

                        @pl.when(who_ref[0] == 0)
                        def _(block=block, start=start, at=at):
                            two_ref[at, start : start + BLK] = block

                    if step == 3:
                        four_ref[at, start + pack - cols : start + pack - cols + BLK] = block

    def like(*shape):
        return jax.ShapeDtypeStruct(shape, coeffs.dtype)

    sources = (coeffs, direction, ham_band, ovl_band, band_mask, local_mask)
    vmem = pl.BlockSpec(memory_space=pltpu.VMEM)
    wide = pack + 2 * rows
    return pl.pallas_call(
        kernel,
        out_shape=(
            like(rows, cols), like(rows, 2 * cols), like(rows, wide), like(rows, wide), like(rows, 2 * rows),
        ),
        in_specs=[pl.BlockSpec(memory_space=pltpu.SMEM)]
        + [pl.BlockSpec(memory_space=pltpu.HBM)] * len(sources),
        out_specs=(vmem,) * 5,
        scratch_shapes=[pltpu.VMEM(source.shape, source.dtype) for source in sources[:4]]
        + [pltpu.SMEM(source.shape, source.dtype) for source in sources[4:]]
        + [pltpu.SemaphoreType.DMA((len(sources),))],
        compiler_params=pltpu.CompilerParams(vmem_limit_bytes=60 * 2**20),
        cost_estimate=pl.CostEstimate(flops=0, bytes_accessed=20 * rows * wide, transcendentals=0),
    )(who, *sources)


def summed_copies(parts, scale, *others):
    def kernel(parts_ref, *refs):
        total = parts_ref[0]
        for i in range(1, parts.shape[0]):
            total = total + parts_ref[i]
        total = total * scale
        for i in range(parts.shape[0]):
            refs[-1][i] = total

    return pl.pallas_call(
        kernel,
        out_shape=jax.ShapeDtypeStruct(parts.shape, parts.dtype),
        in_specs=[pl.BlockSpec(memory_space=pltpu.VMEM)]
        + [pl.BlockSpec(memory_space=pl.ANY)] * len(others),
        out_specs=pl.BlockSpec(memory_space=pltpu.VMEM),
        compiler_params=pltpu.CompilerParams(vmem_limit_bytes=16 * 2**20),
        cost_estimate=pl.CostEstimate(flops=parts.size, bytes_accessed=8 * parts.size, transcendentals=0),
    )(parts, *others)


def on_device(coeffs, direction, ham_diag, ovl_diag, ham_band, ovl_band, band_mask, local_mask):
    rows = coeffs.shape[0]
    cols = coeffs.shape[1]
    basis_total = rows * lax.axis_size(BASIS)
    core = lax.axis_index("c")
    first_core = core == 0
    local_full = expand_mask(local_mask).astype(jnp.bfloat16)
    coeff, stacked, sent_2, sent_4, nearest = prepared(
        jnp.stack([core]).astype(jnp.int32),
        coeffs, direction, ham_band, ovl_band, band_mask, local_mask,
    )

    ahead_2 = shifted(stacked, -2)
    ahead_4 = shifted(stacked, -4)
    behind_2 = shifted(sent_2, 2)
    behind_4 = shifted(sent_4, 4)
    place = lax.axis_index("orb")
    every_coeff = lax.all_gather(after(coeff, stacked, sent_2, sent_4), "orb", axis=0)

    def peer(g):
        return lax.dynamic_index_in_dim(every_coeff, (place + g) % SIZES["orb"], 0, keepdims=False)

    near_peers = [peer(2 * core + k) for k in range(2)]
    pack = cols + 2 * rows
    wanted = [(place + 2 - 2 * core + k) % SIZES["orb"] for k in range(2)]
    who = jnp.stack([core] + wanted).astype(jnp.int32)
    crossed = swapped(
        packed(who, coeff, nearest, behind_2, behind_4, stacked, ahead_2, ahead_4, every_coeff), "c"
    )
    odd_behind = crossed[:, : 2 * pack]
    odd_ahead = crossed[:, 2 * pack : 2 * pack + 4 * cols]
    gram_left = jnp.concatenate(
        [
            jnp.concatenate(near_peers, axis=1),
            crossed[:, 2 * pack + 4 * cols :],
        ],
        axis=0,
    )

    band_full = expand_mask(band_mask).astype(jnp.bfloat16)
    upright = [
        jnp.concatenate(
            [(band * band_full)[:, k * rows : (k + 1) * rows] for band in (ham_band, ovl_band)], axis=0
        )
        for k in range(ham_band.shape[1] // rows)
    ]

    forward = plain_dot(jnp.concatenate([ham_diag, ovl_diag], axis=0), stacked)
    forward = forward + plain_dot(upright[1], ahead_2)
    forward = forward + plain_dot(upright[3], ahead_4)
    forward = forward + plain_dot(upright[0], odd_ahead[:, : 2 * cols])
    forward = forward + plain_dot(upright[2], odd_ahead[:, 2 * cols :])
    back = dot_left(jnp.concatenate([ham_diag, ovl_diag], axis=1), coeff)
    back = back + dot_left(behind_2[:, pack:], behind_2[:, :cols])
    back = back + dot_left(behind_4[:, pack:], behind_4[:, :cols])
    back = back + dot_left(odd_behind[:, cols:pack], odd_behind[:, :cols])
    back = back + dot_left(odd_behind[:, pack + cols :], odd_behind[:, pack : pack + cols])
    ham_c = forward[:rows, :cols] + back[:rows]
    ovl_c = forward[rows:, :cols] + back[rows:] + coeff.astype(jnp.float32)
    both_c = jnp.concatenate([ham_c, ovl_c], axis=1)

    dir_f = direction.astype(jnp.float32)
    ham_line = 2.0 * jnp.sum(dir_f * forward[:rows, cols:], axis=0)
    ovl_line = jnp.sum(dir_f * (2.0 * forward[rows:, cols:] + dir_f), axis=0)

    swapped_c = jnp.concatenate([ovl_c, ham_c], axis=1)
    mid = rows // 2
    next_top, last_bottom = over_orb(swapped_c[:mid], -1), over_orb(swapped_c[mid:], 1)
    next_bottom, last_top = over_orb(swapped_c[mid:], -1), over_orb(swapped_c[:mid], 1)
    other_c = swapped(both_c, "c")

    partial = dot_left(
        gram_left.astype(jnp.float32), jnp.concatenate([both_c, other_c], axis=0), HIGH
    )
    chip_axes = ("y", "z", "x")
    chips = lax.axis_size(chip_axes)
    parts = lax.all_to_all(
        partial.reshape(chips, 2 * cols // chips, 2 * cols), chip_axes, 0, 0
    )
    copies = summed_copies(
        parts, 1.0 / basis_total, next_top[:8, :BLK], last_bottom[:8, :BLK]
    )
    top = over_orb(next_top, -1)
    bottom = over_orb(last_bottom, 1)
    every_c = [
        swapped_c,
        jnp.concatenate([next_top, next_bottom], axis=0),
        after(jnp.concatenate([top, bottom], axis=0), copies),
        jnp.concatenate([last_top, last_bottom], axis=0),
    ]
    half = lax.all_to_all(copies, chip_axes, 0, 0).reshape(2, cols, 2 * cols)
    other_half = swapped(half, "c")
    mixed = jnp.zeros((rows, cols), jnp.float32)
    for near, grams in ((first_core, half), (~first_core, other_half)):
        for k in range(2):
            theirs = jnp.where(near, every_c[k], every_c[2 + k])
            mixed = mixed + plain_dot(theirs[:, :cols], grams[k, :, :cols], HIGH)
            mixed = mixed + plain_dot(theirs[:, cols:], grams[k, :, cols:], HIGH)
    gradient = (4.0 * ham_c - 2.0 * mixed) * local_full.astype(jnp.float32)

    lines = jnp.stack([ham_line, ovl_line, jnp.sum(dir_f * gradient, axis=0)], axis=0)
    lines = lines + swapped(lines, "c")
    copies = jnp.broadcast_to(lines.reshape(1, -1, BLK), (chips, lines.size // BLK, BLK))
    every_line = lax.all_to_all(copies, chip_axes, 0, 0)
    line_terms = jnp.sum(every_line, axis=0).reshape(lines.shape) * (1.0 / math.sqrt(basis_total))
    return (gradient, line_terms)


def solution(mesh):
    fine = Mesh(mesh.devices.reshape(tuple(SIZES.values())), tuple(SIZES))
    placed = (P(BASIS, "orb"), P(BASIS, "orb")) + (P(BASIS, None),) * 5 + (P(BASIS, "orb"),)
    return jax.shard_map(
        on_device,
        mesh=fine,
        in_specs=placed,
        out_specs=(P(BASIS, "orb"), P(None, "orb")),
        check_vma=False,
    )
```

```python
import math

import jax
import jax.numpy as jnp
from jax import lax
from jax.experimental import pallas as pl
from jax.experimental.pallas import tpu as pltpu
from jax.sharding import Mesh, PartitionSpec as P

BLK = 128
BASIS = ("z", "x", "y", "c")
SIZES = {"z": 8, "x": 4, "y": 2, "c": 2, "orb": 4}
HIGH = lax.Precision.HIGH


def shifted(shard, by):
    count = lax.axis_size(BASIS)
    return lax.ppermute(shard, BASIS, [(i, (i + by) % count) for i in range(count)])


def swapped(shard, axis):
    return lax.ppermute(shard, axis, [(0, 1), (1, 0)])


def expand_mask(mask_blocks):
    grown = jnp.repeat(mask_blocks, BLK, axis=0)
    return jnp.repeat(grown, BLK, axis=1)


def plain_dot(left, right, precision=None):
    return jnp.dot(left, right, precision=precision, preferred_element_type=jnp.float32)


def dot_left(left, right, precision=None):
    return lax.dot_general(
        left, right, (((0,), (0,)), ((), ())),
        precision=precision, preferred_element_type=jnp.float32,
    )


def after(shard, *others):
    def nothing(*refs):
        del refs

    return pl.pallas_call(
        nothing,
        out_shape=jax.ShapeDtypeStruct(shard.shape, shard.dtype),
        in_specs=[pl.BlockSpec(memory_space=pl.ANY)] * (1 + len(others)),
        out_specs=pl.BlockSpec(memory_space=pl.ANY),
        input_output_aliases={0: 0},
    )(shard, *others)


def over_orb(shard, by):
    orbs = SIZES["orb"]
    return lax.ppermute(shard, "orb", [(i, (i + by) % orbs) for i in range(orbs)])


def packed(who, coeff, nearest, behind_2, behind_4, stacked, ahead_2, ahead_4, every_coeff):
    rows, cols = coeff.shape
    pack = cols + nearest.shape[1]
    width = 2 * pack + 6 * cols

    def kernel(who_ref, coeff_ref, near_ref, b2_ref, b4_ref, own_ref, a2_ref, a4_ref, all_ref, out_ref):
        @pl.when(who_ref[0] == 0)
        def _():
            out_ref[:, :cols] = coeff_ref[...]
            out_ref[:, cols:pack] = near_ref[...]
            out_ref[:, pack : 2 * pack] = b2_ref[:, :pack]
            out_ref[:, 2 * pack : 2 * pack + 2 * cols] = a2_ref[...]
            out_ref[:, 2 * pack + 2 * cols : 2 * pack + 4 * cols] = a4_ref[...]

        @pl.when(who_ref[0] != 0)
        def _():
            out_ref[:, :pack] = b2_ref[:, :pack]
            out_ref[:, pack : 2 * pack] = b4_ref[:, :pack]
            out_ref[:, 2 * pack : 2 * pack + 2 * cols] = own_ref[...]
            out_ref[:, 2 * pack + 2 * cols : 2 * pack + 4 * cols] = a2_ref[...]

        for k in range(2):
            start = 2 * pack + (4 + k) * cols
            out_ref[:, start : start + cols] = all_ref[who_ref[1 + k]]

    return pl.pallas_call(
        kernel,
        out_shape=jax.ShapeDtypeStruct((rows, width), coeff.dtype),
        in_specs=[pl.BlockSpec(memory_space=pltpu.SMEM)]
        + [pl.BlockSpec(memory_space=pltpu.VMEM)] * 8,
        out_specs=pl.BlockSpec(memory_space=pltpu.VMEM),
        compiler_params=pltpu.CompilerParams(vmem_limit_bytes=16 * 2**20),
        cost_estimate=pl.CostEstimate(flops=0, bytes_accessed=4 * rows * width, transcendentals=0),
    )(who, coeff, nearest, behind_2, behind_4, stacked, ahead_2, ahead_4, every_coeff)


def prepared(who, coeffs, direction, ham_band, ovl_band, band_mask, local_mask):
    rows, cols = coeffs.shape
    reach = ham_band.shape[1] // rows
    pack = cols + 2 * rows

    def kernel(who_ref, *refs):
        sources, outs, held, sems = refs[:6], refs[6:11], refs[11:17], refs[17]
        fetched = [
            pltpu.make_async_copy(source, slot, sems.at[i])
            for i, (source, slot) in enumerate(zip(sources, held))
        ]
        for copy in fetched:
            copy.start()
        for copy in fetched:
            copy.wait()
        c_ref, d_ref, h_ref, s_ref, band_ref, local_ref = held
        coeff_ref, stacked_ref, two_ref, four_ref, near_ref = outs
        for i in range(rows // BLK):
            at = slice(i * BLK, (i + 1) * BLK)
            for j in range(cols // BLK):
                block = c_ref[at, j * BLK : (j + 1) * BLK]
                block = jnp.where(local_ref[i, j] != 0, block, jnp.zeros_like(block))
                for ref in (coeff_ref, stacked_ref, two_ref, four_ref):
                    ref[at, j * BLK : (j + 1) * BLK] = block
            stacked_ref[at, cols:] = d_ref[at, :]
            for j in range(reach * rows // BLK):
                step, within = divmod(j * BLK, rows)
                for m, ref in enumerate((h_ref, s_ref)):
                    block = ref[at, j * BLK : (j + 1) * BLK]
                    block = jnp.where(band_ref[i, j] != 0, block, jnp.zeros_like(block))
                    start = cols + m * rows + within
                    if step == 0:
                        near_ref[at, start - cols : start - cols + BLK] = block

                        @pl.when(who_ref[0] != 0)
                        def _(block=block, start=start, at=at):
                            two_ref[at, start : start + BLK] = block

                    if step == 1:
                        two_ref[at, start + pack - cols : start + pack - cols + BLK] = block
                    if step == 2:
                        four_ref[at, start : start + BLK] = block

                        @pl.when(who_ref[0] == 0)
                        def _(block=block, start=start, at=at):
                            two_ref[at, start : start + BLK] = block

                    if step == 3:
                        four_ref[at, start + pack - cols : start + pack - cols + BLK] = block

    def like(*shape):
        return jax.ShapeDtypeStruct(shape, coeffs.dtype)

    sources = (coeffs, direction, ham_band, ovl_band, band_mask, local_mask)
    vmem = pl.BlockSpec(memory_space=pltpu.VMEM)
    wide = pack + 2 * rows
    return pl.pallas_call(
        kernel,
        out_shape=(
            like(rows, cols), like(rows, 2 * cols), like(rows, wide), like(rows, wide), like(rows, 2 * rows),
        ),
        in_specs=[pl.BlockSpec(memory_space=pltpu.SMEM)]
        + [pl.BlockSpec(memory_space=pltpu.HBM)] * len(sources),
        out_specs=(vmem,) * 5,
        scratch_shapes=[pltpu.VMEM(source.shape, source.dtype) for source in sources[:4]]
        + [pltpu.SMEM(source.shape, source.dtype) for source in sources[4:]]
        + [pltpu.SemaphoreType.DMA((len(sources),))],
        compiler_params=pltpu.CompilerParams(vmem_limit_bytes=60 * 2**20),
        cost_estimate=pl.CostEstimate(flops=0, bytes_accessed=20 * rows * wide, transcendentals=0),
    )(who, *sources)


def summed_copies(parts, scale, *others):
    def kernel(parts_ref, *refs):
        total = parts_ref[0]
        for i in range(1, parts.shape[0]):
            total = total + parts_ref[i]
        total = total * scale
        for i in range(parts.shape[0]):
            refs[-1][i] = total

    return pl.pallas_call(
        kernel,
        out_shape=jax.ShapeDtypeStruct(parts.shape, parts.dtype),
        in_specs=[pl.BlockSpec(memory_space=pltpu.VMEM)]
        + [pl.BlockSpec(memory_space=pl.ANY)] * len(others),
        out_specs=pl.BlockSpec(memory_space=pltpu.VMEM),
        compiler_params=pltpu.CompilerParams(vmem_limit_bytes=16 * 2**20),
        cost_estimate=pl.CostEstimate(flops=parts.size, bytes_accessed=8 * parts.size, transcendentals=0),
    )(parts, *others)


def finished(who, half, other_half, own, others, direction, local_mask):
    rows, wide = own.shape
    cols = wide // 2
    mid = rows // 2

    def split(value):
        high = value.astype(jnp.bfloat16)
        return high, (value - high.astype(jnp.float32)).astype(jnp.bfloat16)

    def kernel(who_ref, half_ref, far_ref, own_ref, *refs):
        other_refs, (d_ref, local_ref, grad_ref, line_ref, high_ref, low_ref) = refs[:6], refs[6:]
        for k in range(2):
            for base, ref in ((2 * who_ref[0], half_ref), (2 - 2 * who_ref[0], far_ref)):
                high, low = split(ref[k])
                high_ref[base + k] = high
                low_ref[base + k] = low
        line = jnp.zeros((1, cols), jnp.float32)
        for i in range(2):
            at = slice(i * mid, (i + 1) * mid)
            total = jnp.zeros((mid, cols), jnp.float32)
            for b in range(4):
                held = own_ref[at, :] if b == 0 else other_refs[2 * b - 2 + i][...]
                high, low = split(held)
                for x in range(2):
                    part = slice(x * cols, (x + 1) * cols)
                    for left, right in ((high, high_ref), (high, low_ref), (low, high_ref)):
                        total = total + jnp.dot(
                            left[:, part], right[b, :, part], preferred_element_type=jnp.float32
                        )
            grad = 4.0 * own_ref[at, cols:] - 2.0 * total
            for j in range(cols // BLK):
                side = slice(j * BLK, (j + 1) * BLK)
                block = grad[:, side]
                grad_ref[at, side] = jnp.where(local_ref[i, j] != 0, block, jnp.zeros_like(block))
            line = line + jnp.sum(
                d_ref[at, :].astype(jnp.float32) * grad_ref[at, :], axis=0, keepdims=True
            )
        line_ref[...] = line

    smem, vmem = pl.BlockSpec(memory_space=pltpu.SMEM), pl.BlockSpec(memory_space=pltpu.VMEM)
    return pl.pallas_call(
        kernel,
        out_shape=(
            jax.ShapeDtypeStruct((rows, cols), jnp.float32), jax.ShapeDtypeStruct((1, cols), jnp.float32),
        ),
        in_specs=[smem] + [vmem] * 10 + [smem],
        out_specs=(vmem, vmem),
        scratch_shapes=[pltpu.VMEM((4, cols, wide), jnp.bfloat16)] * 2,
        compiler_params=pltpu.CompilerParams(vmem_limit_bytes=24 * 2**20),
        cost_estimate=pl.CostEstimate(
            flops=24 * rows * wide * cols, bytes_accessed=20 * rows * wide * 4, transcendentals=0
        ),
    )(who, half, other_half, own, *others, direction, local_mask)


def on_device(coeffs, direction, ham_diag, ovl_diag, ham_band, ovl_band, band_mask, local_mask):
    rows = coeffs.shape[0]
    cols = coeffs.shape[1]
    basis_total = rows * lax.axis_size(BASIS)
    core = lax.axis_index("c")
    first_core = core == 0
    coeff, stacked, sent_2, sent_4, nearest = prepared(
        jnp.stack([core]).astype(jnp.int32),
        coeffs, direction, ham_band, ovl_band, band_mask, local_mask,
    )

    ahead_2 = shifted(stacked, -2)
    ahead_4 = shifted(stacked, -4)
    behind_2 = shifted(sent_2, 2)
    behind_4 = shifted(sent_4, 4)
    place = lax.axis_index("orb")
    every_coeff = lax.all_gather(after(coeff, stacked, sent_2, sent_4), "orb", axis=0)

    def peer(g):
        return lax.dynamic_index_in_dim(every_coeff, (place + g) % SIZES["orb"], 0, keepdims=False)

    near_peers = [peer(2 * core + k) for k in range(2)]
    pack = cols + 2 * rows
    wanted = [(place + 2 - 2 * core + k) % SIZES["orb"] for k in range(2)]
    who = jnp.stack([core] + wanted).astype(jnp.int32)
    crossed = swapped(
        packed(who, coeff, nearest, behind_2, behind_4, stacked, ahead_2, ahead_4, every_coeff), "c"
    )
    odd_behind = crossed[:, : 2 * pack]
    odd_ahead = crossed[:, 2 * pack : 2 * pack + 4 * cols]
    gram_left = jnp.concatenate(
        [
            jnp.concatenate(near_peers, axis=1),
            crossed[:, 2 * pack + 4 * cols :],
        ],
        axis=0,
    )

    band_full = expand_mask(band_mask).astype(jnp.bfloat16)
    upright = [
        jnp.concatenate(
            [(band * band_full)[:, k * rows : (k + 1) * rows] for band in (ham_band, ovl_band)], axis=0
        )
        for k in range(ham_band.shape[1] // rows)
    ]

    forward = plain_dot(jnp.concatenate([ham_diag, ovl_diag], axis=0), stacked)
    forward = forward + plain_dot(upright[1], ahead_2)
    forward = forward + plain_dot(upright[3], ahead_4)
    forward = forward + plain_dot(upright[0], odd_ahead[:, : 2 * cols])
    forward = forward + plain_dot(upright[2], odd_ahead[:, 2 * cols :])
    back = dot_left(jnp.concatenate([ham_diag, ovl_diag], axis=1), coeff)
    back = back + dot_left(behind_2[:, pack:], behind_2[:, :cols])
    back = back + dot_left(behind_4[:, pack:], behind_4[:, :cols])
    back = back + dot_left(odd_behind[:, cols:pack], odd_behind[:, :cols])
    back = back + dot_left(odd_behind[:, pack + cols :], odd_behind[:, pack : pack + cols])
    ham_c = forward[:rows, :cols] + back[:rows]
    ovl_c = forward[rows:, :cols] + back[rows:] + coeff.astype(jnp.float32)
    both_c = jnp.concatenate([ham_c, ovl_c], axis=1)

    dir_f = direction.astype(jnp.float32)
    ham_line = 2.0 * jnp.sum(dir_f * forward[:rows, cols:], axis=0)
    ovl_line = jnp.sum(dir_f * (2.0 * forward[rows:, cols:] + dir_f), axis=0)

    swapped_c = jnp.concatenate([ovl_c, ham_c], axis=1)
    mid = rows // 2
    next_top, last_bottom = over_orb(swapped_c[:mid], -1), over_orb(swapped_c[mid:], 1)
    next_bottom, last_top = over_orb(swapped_c[mid:], -1), over_orb(swapped_c[:mid], 1)
    other_c = swapped(both_c, "c")

    partial = dot_left(
        gram_left.astype(jnp.float32), jnp.concatenate([both_c, other_c], axis=0), HIGH
    )
    chip_axes = ("y", "z", "x")
    chips = lax.axis_size(chip_axes)
    parts = lax.all_to_all(
        partial.reshape(chips, 2 * cols // chips, 2 * cols), chip_axes, 0, 0
    )
    copies = summed_copies(
        parts, 1.0 / basis_total, next_top[:8, :BLK], last_bottom[:8, :BLK]
    )
    top = over_orb(next_top, -1)
    bottom = over_orb(last_bottom, 1)
    half = lax.all_to_all(copies, chip_axes, 0, 0).reshape(2, cols, 2 * cols)
    half, top, bottom, next_bottom, last_top = lax.optimization_barrier(
        (half, top, bottom, next_bottom, last_top)
    )
    other_half = swapped(half, "c")
    gradient, grad_line = finished(
        jnp.stack([core]).astype(jnp.int32), half, other_half, swapped_c,
        [next_top, next_bottom, top, bottom, last_top, last_bottom], direction, local_mask,
    )
    lines = jnp.stack([ham_line, ovl_line, grad_line[0]], axis=0)
    lines = lines + swapped(lines, "c")
    copies = jnp.broadcast_to(lines.reshape(1, -1, BLK), (chips, lines.size // BLK, BLK))
    every_line = lax.all_to_all(copies, chip_axes, 0, 0)
    line_terms = jnp.sum(every_line, axis=0).reshape(lines.shape) * (1.0 / math.sqrt(basis_total))
    return (gradient, line_terms)


def solution(mesh):
    fine = Mesh(mesh.devices.reshape(tuple(SIZES.values())), tuple(SIZES))
    placed = (P(BASIS, "orb"), P(BASIS, "orb")) + (P(BASIS, None),) * 5 + (P(BASIS, "orb"),)
    return jax.shard_map(
        on_device,
        mesh=fine,
        in_specs=placed,
        out_specs=(P(BASIS, "orb"), P(None, "orb")),
        check_vma=False,
    )
```

```python
import math

import jax
import jax.numpy as jnp
from jax import lax
from jax.experimental import pallas as pl
from jax.experimental.pallas import tpu as pltpu
from jax.sharding import Mesh, PartitionSpec as P

BLK = 128
BASIS = ("z", "x", "y", "c")
SIZES = {"z": 8, "x": 4, "y": 2, "c": 2, "orb": 4}
HIGH = lax.Precision.HIGH


def shifted(shard, by):
    count = lax.axis_size(BASIS)
    return lax.ppermute(shard, BASIS, [(i, (i + by) % count) for i in range(count)])


def swapped(shard, axis):
    return lax.ppermute(shard, axis, [(0, 1), (1, 0)])


def expand_mask(mask_blocks):
    grown = jnp.repeat(mask_blocks, BLK, axis=0)
    return jnp.repeat(grown, BLK, axis=1)


def plain_dot(left, right, precision=None):
    return jnp.dot(left, right, precision=precision, preferred_element_type=jnp.float32)


def dot_left(left, right, precision=None):
    return lax.dot_general(
        left, right, (((0,), (0,)), ((), ())),
        precision=precision, preferred_element_type=jnp.float32,
    )


def after(shard, *others):
    def nothing(*refs):
        del refs

    return pl.pallas_call(
        nothing,
        out_shape=jax.ShapeDtypeStruct(shard.shape, shard.dtype),
        in_specs=[pl.BlockSpec(memory_space=pl.ANY)] * (1 + len(others)),
        out_specs=pl.BlockSpec(memory_space=pl.ANY),
        input_output_aliases={0: 0},
    )(shard, *others)


def over_orb(shard, by):
    orbs = SIZES["orb"]
    return lax.ppermute(shard, "orb", [(i, (i + by) % orbs) for i in range(orbs)])


def packed(who, coeff, nearest, behind_2, behind_4, stacked, ahead_2, ahead_4, every_coeff):
    rows, cols = coeff.shape
    pack = cols + nearest.shape[1]
    width = 2 * pack + 6 * cols

    def kernel(who_ref, coeff_ref, near_ref, b2_ref, b4_ref, own_ref, a2_ref, a4_ref, all_ref, out_ref):
        @pl.when(who_ref[0] == 0)
        def _():
            out_ref[:, :cols] = coeff_ref[...]
            out_ref[:, cols:pack] = near_ref[...]
            out_ref[:, pack : 2 * pack] = b2_ref[:, :pack]
            out_ref[:, 2 * pack : 2 * pack + 2 * cols] = a2_ref[...]
            out_ref[:, 2 * pack + 2 * cols : 2 * pack + 4 * cols] = a4_ref[...]

        @pl.when(who_ref[0] != 0)
        def _():
            out_ref[:, :pack] = b2_ref[:, :pack]
            out_ref[:, pack : 2 * pack] = b4_ref[:, :pack]
            out_ref[:, 2 * pack : 2 * pack + 2 * cols] = own_ref[...]
            out_ref[:, 2 * pack + 2 * cols : 2 * pack + 4 * cols] = a2_ref[...]

        for k in range(2):
            start = 2 * pack + (4 + k) * cols
            out_ref[:, start : start + cols] = all_ref[who_ref[1 + k]]

    return pl.pallas_call(
        kernel,
        out_shape=jax.ShapeDtypeStruct((rows, width), coeff.dtype),
        in_specs=[pl.BlockSpec(memory_space=pltpu.SMEM)]
        + [pl.BlockSpec(memory_space=pltpu.VMEM)] * 8,
        out_specs=pl.BlockSpec(memory_space=pltpu.VMEM),
        compiler_params=pltpu.CompilerParams(vmem_limit_bytes=16 * 2**20),
        cost_estimate=pl.CostEstimate(flops=0, bytes_accessed=4 * rows * width, transcendentals=0),
    )(who, coeff, nearest, behind_2, behind_4, stacked, ahead_2, ahead_4, every_coeff)


def prepared(who, coeffs, direction, ham_band, ovl_band, band_mask, local_mask):
    rows, cols = coeffs.shape
    reach = ham_band.shape[1] // rows
    pack = cols + 2 * rows

    def kernel(who_ref, *refs):
        sources, outs, held, sems = refs[:6], refs[6:11], refs[11:17], refs[17]
        fetched = [
            pltpu.make_async_copy(source, slot, sems.at[i])
            for i, (source, slot) in enumerate(zip(sources, held))
        ]
        for copy in fetched:
            copy.start()
        for copy in fetched:
            copy.wait()
        c_ref, d_ref, h_ref, s_ref, band_ref, local_ref = held
        coeff_ref, stacked_ref, two_ref, four_ref, near_ref = outs
        for i in range(rows // BLK):
            at = slice(i * BLK, (i + 1) * BLK)
            for j in range(cols // BLK):
                block = c_ref[at, j * BLK : (j + 1) * BLK]
                block = jnp.where(local_ref[i, j] != 0, block, jnp.zeros_like(block))
                for ref in (coeff_ref, stacked_ref, two_ref, four_ref):
                    ref[at, j * BLK : (j + 1) * BLK] = block
            stacked_ref[at, cols:] = d_ref[at, :]
            for j in range(reach * rows // BLK):
                step, within = divmod(j * BLK, rows)
                for m, ref in enumerate((h_ref, s_ref)):
                    block = ref[at, j * BLK : (j + 1) * BLK]
                    block = jnp.where(band_ref[i, j] != 0, block, jnp.zeros_like(block))
                    start = cols + m * rows + within
                    if step == 0:
                        near_ref[at, start - cols : start - cols + BLK] = block

                        @pl.when(who_ref[0] != 0)
                        def _(block=block, start=start, at=at):
                            two_ref[at, start : start + BLK] = block

                    if step == 1:
                        two_ref[at, start + pack - cols : start + pack - cols + BLK] = block
                    if step == 2:
                        four_ref[at, start : start + BLK] = block

                        @pl.when(who_ref[0] == 0)
                        def _(block=block, start=start, at=at):
                            two_ref[at, start : start + BLK] = block

                    if step == 3:
                        four_ref[at, start + pack - cols : start + pack - cols + BLK] = block

    def like(*shape):
        return jax.ShapeDtypeStruct(shape, coeffs.dtype)

    sources = (coeffs, direction, ham_band, ovl_band, band_mask, local_mask)
    vmem = pl.BlockSpec(memory_space=pltpu.VMEM)
    wide = pack + 2 * rows
    return pl.pallas_call(
        kernel,
        out_shape=(
            like(rows, cols), like(rows, 2 * cols), like(rows, wide), like(rows, wide), like(rows, 2 * rows),
        ),
        in_specs=[pl.BlockSpec(memory_space=pltpu.SMEM)]
        + [pl.BlockSpec(memory_space=pltpu.HBM)] * len(sources),
        out_specs=(vmem,) * 5,
        scratch_shapes=[pltpu.VMEM(source.shape, source.dtype) for source in sources[:4]]
        + [pltpu.SMEM(source.shape, source.dtype) for source in sources[4:]]
        + [pltpu.SemaphoreType.DMA((len(sources),))],
        compiler_params=pltpu.CompilerParams(vmem_limit_bytes=60 * 2**20),
        cost_estimate=pl.CostEstimate(flops=0, bytes_accessed=20 * rows * wide, transcendentals=0),
    )(who, *sources)


def summed_copies(parts, scale, *others):
    def kernel(parts_ref, *refs):
        total = parts_ref[0]
        for i in range(1, parts.shape[0]):
            total = total + parts_ref[i]
        total = total * scale
        for i in range(parts.shape[0]):
            refs[-1][i] = total

    return pl.pallas_call(
        kernel,
        out_shape=jax.ShapeDtypeStruct(parts.shape, parts.dtype),
        in_specs=[pl.BlockSpec(memory_space=pltpu.VMEM)]
        + [pl.BlockSpec(memory_space=pl.ANY)] * len(others),
        out_specs=pl.BlockSpec(memory_space=pltpu.VMEM),
        compiler_params=pltpu.CompilerParams(vmem_limit_bytes=16 * 2**20),
        cost_estimate=pl.CostEstimate(flops=parts.size, bytes_accessed=8 * parts.size, transcendentals=0),
    )(parts, *others)


def finished(who, half, other_half, own, others, direction, local_mask):
    rows, wide = own.shape
    cols = wide // 2
    mid = rows // 2

    def split(value):
        high = value.astype(jnp.bfloat16)
        return high, (value - high.astype(jnp.float32)).astype(jnp.bfloat16)

    def kernel(who_ref, half_ref, far_ref, own_ref, *refs):
        other_refs, (d_ref, local_ref, grad_ref, line_ref, high_ref, low_ref) = refs[:6], refs[6:]
        for k in range(2):
            for base, ref in ((2 * who_ref[0], half_ref), (2 - 2 * who_ref[0], far_ref)):
                high, low = split(ref[k])
                high_ref[base + k] = high
                low_ref[base + k] = low
        line = jnp.zeros((1, cols), jnp.float32)
        for i in range(2):
            at = slice(i * mid, (i + 1) * mid)
            total = jnp.zeros((mid, cols), jnp.float32)
            for b in range(4):
                held = own_ref[at, :] if b == 0 else other_refs[2 * b - 2 + i][...]
                high, low = split(held)
                for x in range(2):
                    part = slice(x * cols, (x + 1) * cols)
                    for left, right in ((high, high_ref), (high, low_ref), (low, high_ref)):
                        total = total + jnp.dot(
                            left[:, part], right[b, :, part], preferred_element_type=jnp.float32
                        )
            grad = 4.0 * own_ref[at, cols:] - 2.0 * total
            for j in range(cols // BLK):
                side = slice(j * BLK, (j + 1) * BLK)
                block = grad[:, side]
                grad_ref[at, side] = jnp.where(local_ref[i, j] != 0, block, jnp.zeros_like(block))
            line = line + jnp.sum(
                d_ref[at, :].astype(jnp.float32) * grad_ref[at, :], axis=0, keepdims=True
            )
        line_ref[...] = line

    smem, vmem = pl.BlockSpec(memory_space=pltpu.SMEM), pl.BlockSpec(memory_space=pltpu.VMEM)
    return pl.pallas_call(
        kernel,
        out_shape=(
            jax.ShapeDtypeStruct((rows, cols), jnp.float32), jax.ShapeDtypeStruct((1, cols), jnp.float32),
        ),
        in_specs=[smem] + [vmem] * 10 + [smem],
        out_specs=(vmem, vmem),
        scratch_shapes=[pltpu.VMEM((4, cols, wide), jnp.bfloat16)] * 2,
        compiler_params=pltpu.CompilerParams(vmem_limit_bytes=24 * 2**20),
        cost_estimate=pl.CostEstimate(
            flops=24 * rows * wide * cols, bytes_accessed=20 * rows * wide * 4, transcendentals=0
        ),
    )(who, half, other_half, own, *others, direction, local_mask)


def on_device(coeffs, direction, ham_diag, ovl_diag, ham_band, ovl_band, band_mask, local_mask):
    rows = coeffs.shape[0]
    cols = coeffs.shape[1]
    basis_total = rows * lax.axis_size(BASIS)
    core = lax.axis_index("c")
    first_core = core == 0
    coeff, stacked, sent_2, sent_4, nearest = prepared(
        jnp.stack([core]).astype(jnp.int32),
        coeffs, direction, ham_band, ovl_band, band_mask, local_mask,
    )

    ahead_2 = shifted(stacked, -2)
    ahead_4 = shifted(stacked, -4)
    behind_2 = shifted(sent_2, 2)
    behind_4 = shifted(sent_4, 4)
    place = lax.axis_index("orb")
    every_coeff = lax.all_gather(after(coeff, stacked, sent_2, sent_4), "orb", axis=0)

    def peer(g):
        return lax.dynamic_index_in_dim(every_coeff, (place + g) % SIZES["orb"], 0, keepdims=False)

    near_peers = [peer(2 * core + k) for k in range(2)]
    pack = cols + 2 * rows
    wanted = [(place + 2 - 2 * core + k) % SIZES["orb"] for k in range(2)]
    who = jnp.stack([core] + wanted).astype(jnp.int32)
    crossed = swapped(
        packed(who, coeff, nearest, behind_2, behind_4, stacked, ahead_2, ahead_4, every_coeff), "c"
    )
    odd_behind = crossed[:, : 2 * pack]
    odd_ahead = crossed[:, 2 * pack : 2 * pack + 4 * cols]
    gram_left = jnp.concatenate(
        [
            jnp.concatenate(near_peers, axis=1),
            crossed[:, 2 * pack + 4 * cols :],
        ],
        axis=0,
    )

    band_full = expand_mask(band_mask).astype(jnp.bfloat16)
    upright = [
        jnp.concatenate(
            [(band * band_full)[:, k * rows : (k + 1) * rows] for band in (ham_band, ovl_band)], axis=0
        )
        for k in range(ham_band.shape[1] // rows)
    ]

    forward = plain_dot(jnp.concatenate([ham_diag, ovl_diag], axis=0), stacked)
    forward = forward + plain_dot(upright[1], ahead_2)
    forward = forward + plain_dot(upright[3], ahead_4)
    forward = forward + plain_dot(upright[0], odd_ahead[:, : 2 * cols])
    forward = forward + plain_dot(upright[2], odd_ahead[:, 2 * cols :])
    back = dot_left(jnp.concatenate([ham_diag, ovl_diag], axis=1), coeff)
    back = back + dot_left(behind_2[:, pack:], behind_2[:, :cols])
    back = back + dot_left(behind_4[:, pack:], behind_4[:, :cols])
    back = back + dot_left(odd_behind[:, cols:pack], odd_behind[:, :cols])
    back = back + dot_left(odd_behind[:, pack + cols :], odd_behind[:, pack : pack + cols])
    ham_c = forward[:rows, :cols] + back[:rows]
    ovl_c = forward[rows:, :cols] + back[rows:] + coeff.astype(jnp.float32)
    both_c = jnp.concatenate([ham_c, ovl_c], axis=1)

    dir_f = direction.astype(jnp.float32)
    ham_line = 2.0 * jnp.sum(dir_f * forward[:rows, cols:], axis=0)
    ovl_line = jnp.sum(dir_f * (2.0 * forward[rows:, cols:] + dir_f), axis=0)

    swapped_c = jnp.concatenate([ovl_c, ham_c], axis=1)
    mid = rows // 2
    next_top, last_bottom = over_orb(swapped_c[:mid], -1), over_orb(swapped_c[mid:], 1)
    next_bottom, last_top = over_orb(swapped_c[mid:], -1), over_orb(swapped_c[:mid], 1)
    other_c = swapped(both_c, "c")

    partial = dot_left(
        gram_left.astype(jnp.float32), jnp.concatenate([both_c, other_c], axis=0), HIGH
    )
    chip_axes = ("y", "z", "x")
    chips = lax.axis_size(chip_axes)
    parts = lax.all_to_all(
        partial.reshape(chips, 2 * cols // chips, 2 * cols), chip_axes, 0, 0
    )
    copies = summed_copies(
        parts, 1.0 / basis_total, next_top[:8, :BLK], last_bottom[:8, :BLK]
    )
    top = over_orb(next_top, -1)
    bottom = over_orb(last_bottom, 1)
    half = lax.all_to_all(copies, chip_axes, 0, 0).reshape(2, cols, 2 * cols)
    half, top, bottom, next_bottom, last_top = lax.optimization_barrier(
        (half, top, bottom, next_bottom, last_top)
    )
    other_half = swapped(half, "c")
    gradient, grad_line = finished(
        jnp.stack([core]).astype(jnp.int32), half, other_half, swapped_c,
        [next_top, next_bottom, top, bottom, last_top, last_bottom], direction, local_mask,
    )
    lines = jnp.stack([ham_line, ovl_line, grad_line[0]], axis=0)
    devices = lax.axis_size(BASIS)
    copies = jnp.broadcast_to(lines.reshape(1, -1, BLK), (devices, lines.size // BLK, BLK))
    every_line = lax.all_to_all(copies, BASIS, 0, 0)
    line_terms = jnp.sum(every_line, axis=0).reshape(lines.shape) * (1.0 / math.sqrt(basis_total))
    return (gradient, line_terms)


def solution(mesh):
    fine = Mesh(mesh.devices.reshape(tuple(SIZES.values())), tuple(SIZES))
    placed = (P(BASIS, "orb"), P(BASIS, "orb")) + (P(BASIS, None),) * 5 + (P(BASIS, "orb"),)
    return jax.shard_map(
        on_device,
        mesh=fine,
        in_specs=placed,
        out_specs=(P(BASIS, "orb"), P(None, "orb")),
        check_vma=False,
    )
```

```python
import math

import jax
import jax.numpy as jnp
from jax import lax
from jax.experimental import pallas as pl
from jax.experimental.pallas import tpu as pltpu
from jax.sharding import Mesh, PartitionSpec as P

BLK = 128
BASIS = ("z", "x", "y", "c")
SIZES = {"z": 8, "x": 4, "y": 2, "c": 2, "orb": 4}
HIGH = lax.Precision.HIGH


def shifted(shard, by):
    count = lax.axis_size(BASIS)
    return lax.ppermute(shard, BASIS, [(i, (i + by) % count) for i in range(count)])


def swapped(shard, axis):
    return lax.ppermute(shard, axis, [(0, 1), (1, 0)])


def expand_mask(mask_blocks):
    grown = jnp.repeat(mask_blocks, BLK, axis=0)
    return jnp.repeat(grown, BLK, axis=1)


def plain_dot(left, right, precision=None):
    return jnp.dot(left, right, precision=precision, preferred_element_type=jnp.float32)


def dot_left(left, right, precision=None):
    return lax.dot_general(
        left, right, (((0,), (0,)), ((), ())),
        precision=precision, preferred_element_type=jnp.float32,
    )


def after(shard, *others):
    def nothing(*refs):
        del refs

    return pl.pallas_call(
        nothing,
        out_shape=jax.ShapeDtypeStruct(shard.shape, shard.dtype),
        in_specs=[pl.BlockSpec(memory_space=pl.ANY)] * (1 + len(others)),
        out_specs=pl.BlockSpec(memory_space=pl.ANY),
        input_output_aliases={0: 0},
    )(shard, *others)


def over_orb(shard, by):
    orbs = SIZES["orb"]
    return lax.ppermute(shard, "orb", [(i, (i + by) % orbs) for i in range(orbs)])


def packed(who, coeff, nearest, behind_2, behind_4, stacked, ahead_2, ahead_4, every_coeff):
    rows, cols = coeff.shape
    pack = cols + nearest.shape[1]
    width = 2 * pack + 6 * cols

    def kernel(who_ref, coeff_ref, near_ref, b2_ref, b4_ref, own_ref, a2_ref, a4_ref, all_ref, out_ref):
        @pl.when(who_ref[0] == 0)
        def _():
            out_ref[:, :cols] = coeff_ref[...]
            out_ref[:, cols:pack] = near_ref[...]
            out_ref[:, pack : 2 * pack] = b2_ref[:, :pack]
            out_ref[:, 2 * pack : 2 * pack + 2 * cols] = a2_ref[...]
            out_ref[:, 2 * pack + 2 * cols : 2 * pack + 4 * cols] = a4_ref[...]

        @pl.when(who_ref[0] != 0)
        def _():
            out_ref[:, :pack] = b2_ref[:, :pack]
            out_ref[:, pack : 2 * pack] = b4_ref[:, :pack]
            out_ref[:, 2 * pack : 2 * pack + 2 * cols] = own_ref[...]
            out_ref[:, 2 * pack + 2 * cols : 2 * pack + 4 * cols] = a2_ref[...]

        for k in range(2):
            start = 2 * pack + (4 + k) * cols
            out_ref[:, start : start + cols] = all_ref[who_ref[1 + k]]

    return pl.pallas_call(
        kernel,
        out_shape=jax.ShapeDtypeStruct((rows, width), coeff.dtype),
        in_specs=[pl.BlockSpec(memory_space=pltpu.SMEM)]
        + [pl.BlockSpec(memory_space=pltpu.VMEM)] * 8,
        out_specs=pl.BlockSpec(memory_space=pltpu.VMEM),
        compiler_params=pltpu.CompilerParams(vmem_limit_bytes=16 * 2**20),
        cost_estimate=pl.CostEstimate(flops=0, bytes_accessed=4 * rows * width, transcendentals=0),
    )(who, coeff, nearest, behind_2, behind_4, stacked, ahead_2, ahead_4, every_coeff)


def prepared(who, coeffs, direction, ham_band, ovl_band, band_mask, local_mask):
    rows, cols = coeffs.shape
    reach = ham_band.shape[1] // rows
    pack = cols + 2 * rows

    def kernel(who_ref, *refs):
        sources, outs, held, sems = refs[:6], refs[6:11], refs[11:17], refs[17]
        fetched = [
            pltpu.make_async_copy(source, slot, sems.at[i])
            for i, (source, slot) in enumerate(zip(sources, held))
        ]
        for copy in fetched:
            copy.start()
        for copy in fetched:
            copy.wait()
        c_ref, d_ref, h_ref, s_ref, band_ref, local_ref = held
        coeff_ref, stacked_ref, two_ref, four_ref, near_ref = outs
        for i in range(rows // BLK):
            at = slice(i * BLK, (i + 1) * BLK)
            for j in range(cols // BLK):
                block = c_ref[at, j * BLK : (j + 1) * BLK]
                block = jnp.where(local_ref[i, j] != 0, block, jnp.zeros_like(block))
                for ref in (coeff_ref, stacked_ref, two_ref, four_ref):
                    ref[at, j * BLK : (j + 1) * BLK] = block
            stacked_ref[at, cols:] = d_ref[at, :]
            for j in range(reach * rows // BLK):
                step, within = divmod(j * BLK, rows)
                for m, ref in enumerate((h_ref, s_ref)):
                    block = ref[at, j * BLK : (j + 1) * BLK]
                    block = jnp.where(band_ref[i, j] != 0, block, jnp.zeros_like(block))
                    start = cols + m * rows + within
                    if step == 0:
                        near_ref[at, start - cols : start - cols + BLK] = block

                        @pl.when(who_ref[0] != 0)
                        def _(block=block, start=start, at=at):
                            two_ref[at, start : start + BLK] = block

                    if step == 1:
                        two_ref[at, start + pack - cols : start + pack - cols + BLK] = block
                    if step == 2:
                        four_ref[at, start : start + BLK] = block

                        @pl.when(who_ref[0] == 0)
                        def _(block=block, start=start, at=at):
                            two_ref[at, start : start + BLK] = block

                    if step == 3:
                        four_ref[at, start + pack - cols : start + pack - cols + BLK] = block

    def like(*shape):
        return jax.ShapeDtypeStruct(shape, coeffs.dtype)

    sources = (coeffs, direction, ham_band, ovl_band, band_mask, local_mask)
    vmem = pl.BlockSpec(memory_space=pltpu.VMEM)
    wide = pack + 2 * rows
    return pl.pallas_call(
        kernel,
        out_shape=(
            like(rows, cols), like(rows, 2 * cols), like(rows, wide), like(rows, wide), like(rows, 2 * rows),
        ),
        in_specs=[pl.BlockSpec(memory_space=pltpu.SMEM)]
        + [pl.BlockSpec(memory_space=pltpu.HBM)] * len(sources),
        out_specs=(vmem,) * 5,
        scratch_shapes=[pltpu.VMEM(source.shape, source.dtype) for source in sources[:4]]
        + [pltpu.SMEM(source.shape, source.dtype) for source in sources[4:]]
        + [pltpu.SemaphoreType.DMA((len(sources),))],
        compiler_params=pltpu.CompilerParams(vmem_limit_bytes=60 * 2**20),
        cost_estimate=pl.CostEstimate(flops=0, bytes_accessed=20 * rows * wide, transcendentals=0),
    )(who, *sources)


def summed_copies(parts, scale, *others):
    def kernel(parts_ref, *refs):
        total = parts_ref[0]
        for i in range(1, parts.shape[0]):
            total = total + parts_ref[i]
        total = total * scale
        for i in range(parts.shape[0]):
            refs[-1][i] = total

    return pl.pallas_call(
        kernel,
        out_shape=jax.ShapeDtypeStruct(parts.shape, parts.dtype),
        in_specs=[pl.BlockSpec(memory_space=pltpu.VMEM)]
        + [pl.BlockSpec(memory_space=pl.ANY)] * len(others),
        out_specs=pl.BlockSpec(memory_space=pltpu.VMEM),
        compiler_params=pltpu.CompilerParams(vmem_limit_bytes=16 * 2**20),
        cost_estimate=pl.CostEstimate(flops=parts.size, bytes_accessed=8 * parts.size, transcendentals=0),
    )(parts, *others)


def finished(who, half, other_half, own, others, direction, local_mask):
    rows, wide = own.shape
    cols = wide // 2
    mid = rows // 2

    def split(value):
        high = value.astype(jnp.bfloat16)
        return high, (value - high.astype(jnp.float32)).astype(jnp.bfloat16)

    def kernel(who_ref, half_ref, far_ref, own_ref, *refs):
        other_refs, (d_ref, local_ref, grad_ref, line_ref, high_ref, low_ref) = refs[:6], refs[6:]
        for k in range(2):
            for base, ref in ((2 * who_ref[0], half_ref), (2 - 2 * who_ref[0], far_ref)):
                high, low = split(ref[k])
                high_ref[base + k] = high
                low_ref[base + k] = low
        line = jnp.zeros((1, cols), jnp.float32)
        for i in range(2):
            at = slice(i * mid, (i + 1) * mid)
            total = jnp.zeros((mid, cols), jnp.float32)
            for b in range(4):
                held = own_ref[at, :] if b == 0 else other_refs[2 * b - 2 + i][...]
                high, low = split(held)
                for x in range(2):
                    part = slice(x * cols, (x + 1) * cols)
                    for left, right in ((high, high_ref), (high, low_ref), (low, high_ref)):
                        total = total + jnp.dot(
                            left[:, part], right[b, :, part], preferred_element_type=jnp.float32
                        )
            grad = 4.0 * own_ref[at, cols:] - 2.0 * total
            for j in range(cols // BLK):
                side = slice(j * BLK, (j + 1) * BLK)
                block = grad[:, side]
                grad_ref[at, side] = jnp.where(local_ref[i, j] != 0, block, jnp.zeros_like(block))
            line = line + jnp.sum(
                d_ref[at, :].astype(jnp.float32) * grad_ref[at, :], axis=0, keepdims=True
            )
        line_ref[...] = line

    smem, vmem = pl.BlockSpec(memory_space=pltpu.SMEM), pl.BlockSpec(memory_space=pltpu.VMEM)
    return pl.pallas_call(
        kernel,
        out_shape=(
            jax.ShapeDtypeStruct((rows, cols), jnp.float32), jax.ShapeDtypeStruct((1, cols), jnp.float32),
        ),
        in_specs=[smem] + [vmem] * 10 + [smem],
        out_specs=(vmem, vmem),
        scratch_shapes=[pltpu.VMEM((4, cols, wide), jnp.bfloat16)] * 2,
        compiler_params=pltpu.CompilerParams(vmem_limit_bytes=24 * 2**20),
        cost_estimate=pl.CostEstimate(
            flops=24 * rows * wide * cols, bytes_accessed=20 * rows * wide * 4, transcendentals=0
        ),
    )(who, half, other_half, own, *others, direction, local_mask)


def on_device(coeffs, direction, ham_diag, ovl_diag, ham_band, ovl_band, band_mask, local_mask):
    rows = coeffs.shape[0]
    cols = coeffs.shape[1]
    basis_total = rows * lax.axis_size(BASIS)
    core = lax.axis_index("c")
    first_core = core == 0
    coeff, stacked, sent_2, sent_4, nearest = prepared(
        jnp.stack([core]).astype(jnp.int32),
        coeffs, direction, ham_band, ovl_band, band_mask, local_mask,
    )

    ahead_2 = shifted(stacked, -2)
    ahead_4 = shifted(stacked, -4)
    behind_2 = shifted(sent_2, 2)
    behind_4 = shifted(sent_4, 4)
    place = lax.axis_index("orb")
    every_coeff = lax.all_gather(after(coeff, stacked, sent_2, sent_4), "orb", axis=0)

    def peer(g):
        return lax.dynamic_index_in_dim(every_coeff, (place + g) % SIZES["orb"], 0, keepdims=False)

    near_peers = [peer(2 * core + k) for k in range(2)]
    pack = cols + 2 * rows
    wanted = [(place + 2 - 2 * core + k) % SIZES["orb"] for k in range(2)]
    who = jnp.stack([core] + wanted).astype(jnp.int32)
    crossed = swapped(
        packed(who, coeff, nearest, behind_2, behind_4, stacked, ahead_2, ahead_4, every_coeff), "c"
    )
    odd_behind = crossed[:, : 2 * pack]
    odd_ahead = crossed[:, 2 * pack : 2 * pack + 4 * cols]
    gram_left = jnp.concatenate(
        [
            jnp.concatenate(near_peers, axis=1),
            crossed[:, 2 * pack + 4 * cols :],
        ],
        axis=0,
    )

    band_full = expand_mask(band_mask).astype(jnp.bfloat16)
    upright = [
        jnp.concatenate(
            [(band * band_full)[:, k * rows : (k + 1) * rows] for band in (ham_band, ovl_band)], axis=0
        )
        for k in range(ham_band.shape[1] // rows)
    ]

    forward = plain_dot(jnp.concatenate([ham_diag, ovl_diag], axis=0), stacked)
    forward = forward + plain_dot(upright[1], ahead_2)
    forward = forward + plain_dot(upright[3], ahead_4)
    forward = forward + plain_dot(upright[0], odd_ahead[:, : 2 * cols])
    forward = forward + plain_dot(upright[2], odd_ahead[:, 2 * cols :])
    back = dot_left(jnp.concatenate([ham_diag, ovl_diag], axis=1), coeff)
    back = back + dot_left(behind_2[:, pack:], behind_2[:, :cols])
    back = back + dot_left(behind_4[:, pack:], behind_4[:, :cols])
    back = back + dot_left(odd_behind[:, cols:pack], odd_behind[:, :cols])
    back = back + dot_left(odd_behind[:, pack + cols :], odd_behind[:, pack : pack + cols])
    ham_c = forward[:rows, :cols] + back[:rows]
    ovl_c = forward[rows:, :cols] + back[rows:] + coeff.astype(jnp.float32)
    both_c = jnp.concatenate([ham_c, ovl_c], axis=1)

    dir_f = direction.astype(jnp.float32)
    ham_line = 2.0 * jnp.sum(dir_f * forward[:rows, cols:], axis=0)
    ovl_line = jnp.sum(dir_f * (2.0 * forward[rows:, cols:] + dir_f), axis=0)

    swapped_c = jnp.concatenate([ovl_c, ham_c], axis=1)
    mid = rows // 2
    next_top, last_bottom = over_orb(swapped_c[:mid], -1), over_orb(swapped_c[mid:], 1)
    next_bottom, last_top = over_orb(swapped_c[mid:], -1), over_orb(swapped_c[:mid], 1)
    other_c = swapped(both_c, "c")

    partial = dot_left(
        gram_left.astype(jnp.float32), jnp.concatenate([both_c, other_c], axis=0), HIGH
    )
    chip_axes = ("y", "z", "x")
    chips = lax.axis_size(chip_axes)
    strips = lax.axis_size(("z", "x"))
    parts = lax.all_to_all(
        partial.reshape(chips, 2 * cols // chips, 2 * cols), chip_axes, 0, 0
    )
    copies = summed_copies(
        parts, 1.0 / basis_total, next_top[:8, :BLK], last_bottom[:8, :BLK]
    )
    top = over_orb(next_top, -1)
    bottom = over_orb(last_bottom, 1)
    half = lax.all_to_all(copies, chip_axes, 0, 0).reshape(2, cols, 2 * cols)
    half, top, bottom, next_bottom, last_top = lax.optimization_barrier(
        (half, top, bottom, next_bottom, last_top)
    )
    other_half = swapped(half, "c")
    gradient, grad_line = finished(
        jnp.stack([core]).astype(jnp.int32), half, other_half, swapped_c,
        [next_top, next_bottom, top, bottom, last_top, last_bottom], direction, local_mask,
    )
    lines = jnp.stack([ham_line, ovl_line, grad_line[0]], axis=0)
    lines = lines + swapped(lines, "c")
    lines = lines + swapped(lines, "y")
    copies = jnp.broadcast_to(lines.reshape(1, -1, BLK), (strips, lines.size // BLK, BLK))
    every_line = lax.all_to_all(copies, ("z", "x"), 0, 0)
    line_terms = jnp.sum(every_line, axis=0).reshape(lines.shape) * (1.0 / math.sqrt(basis_total))
    return (gradient, line_terms)


def solution(mesh):
    fine = Mesh(mesh.devices.reshape(tuple(SIZES.values())), tuple(SIZES))
    placed = (P(BASIS, "orb"), P(BASIS, "orb")) + (P(BASIS, None),) * 5 + (P(BASIS, "orb"),)
    return jax.shard_map(
        on_device,
        mesh=fine,
        in_specs=placed,
        out_specs=(P(BASIS, "orb"), P(None, "orb")),
        check_vma=False,
    )
```

```python
import math

import jax
import jax.numpy as jnp
from jax import lax
from jax.experimental import pallas as pl
from jax.experimental.pallas import tpu as pltpu
from jax.sharding import Mesh, PartitionSpec as P

BLK = 128
BASIS = ("z", "x", "y", "c")
SIZES = {"z": 8, "x": 4, "y": 2, "c": 2, "orb": 4}
HIGH = lax.Precision.HIGH


def shifted(shard, by):
    count = lax.axis_size(BASIS)
    return lax.ppermute(shard, BASIS, [(i, (i + by) % count) for i in range(count)])


def swapped(shard, axis):
    return lax.ppermute(shard, axis, [(0, 1), (1, 0)])


def expand_mask(mask_blocks):
    grown = jnp.repeat(mask_blocks, BLK, axis=0)
    return jnp.repeat(grown, BLK, axis=1)


def plain_dot(left, right, precision=None):
    return jnp.dot(left, right, precision=precision, preferred_element_type=jnp.float32)


def dot_left(left, right, precision=None):
    return lax.dot_general(
        left, right, (((0,), (0,)), ((), ())),
        precision=precision, preferred_element_type=jnp.float32,
    )


def after(shard, *others):
    def nothing(*refs):
        del refs

    return pl.pallas_call(
        nothing,
        out_shape=jax.ShapeDtypeStruct(shard.shape, shard.dtype),
        in_specs=[pl.BlockSpec(memory_space=pl.ANY)] * (1 + len(others)),
        out_specs=pl.BlockSpec(memory_space=pl.ANY),
        input_output_aliases={0: 0},
    )(shard, *others)


def over_orb(shard, by):
    orbs = SIZES["orb"]
    return lax.ppermute(shard, "orb", [(i, (i + by) % orbs) for i in range(orbs)])


def packed(who, coeff, nearest, behind_2, behind_4, stacked, ahead_2, ahead_4, every_coeff):
    rows, cols = coeff.shape
    pack = cols + nearest.shape[1]
    width = 2 * pack + 6 * cols

    def kernel(who_ref, coeff_ref, near_ref, b2_ref, b4_ref, own_ref, a2_ref, a4_ref, all_ref, out_ref):
        @pl.when(who_ref[0] == 0)
        def _():
            out_ref[:, :cols] = coeff_ref[...]
            out_ref[:, cols:pack] = near_ref[...]
            out_ref[:, pack : 2 * pack] = b2_ref[:, :pack]
            out_ref[:, 2 * pack : 2 * pack + 2 * cols] = a2_ref[...]
            out_ref[:, 2 * pack + 2 * cols : 2 * pack + 4 * cols] = a4_ref[...]

        @pl.when(who_ref[0] != 0)
        def _():
            out_ref[:, :pack] = b2_ref[:, :pack]
            out_ref[:, pack : 2 * pack] = b4_ref[:, :pack]
            out_ref[:, 2 * pack : 2 * pack + 2 * cols] = own_ref[...]
            out_ref[:, 2 * pack + 2 * cols : 2 * pack + 4 * cols] = a2_ref[...]

        for k in range(2):
            start = 2 * pack + (4 + k) * cols
            out_ref[:, start : start + cols] = all_ref[who_ref[1 + k]]

    return pl.pallas_call(
        kernel,
        out_shape=jax.ShapeDtypeStruct((rows, width), coeff.dtype),
        in_specs=[pl.BlockSpec(memory_space=pltpu.SMEM)]
        + [pl.BlockSpec(memory_space=pltpu.VMEM)] * 8,
        out_specs=pl.BlockSpec(memory_space=pltpu.VMEM),
        compiler_params=pltpu.CompilerParams(vmem_limit_bytes=16 * 2**20),
        cost_estimate=pl.CostEstimate(flops=0, bytes_accessed=4 * rows * width, transcendentals=0),
    )(who, coeff, nearest, behind_2, behind_4, stacked, ahead_2, ahead_4, every_coeff)


def prepared(who, coeffs, direction, ham_band, ovl_band, band_mask, local_mask):
    rows, cols = coeffs.shape
    reach = ham_band.shape[1] // rows
    pack = cols + 2 * rows

    def kernel(who_ref, *refs):
        sources, outs, held, sems = refs[:6], refs[6:11], refs[11:17], refs[17]
        fetched = [
            pltpu.make_async_copy(source, slot, sems.at[i])
            for i, (source, slot) in enumerate(zip(sources, held))
        ]
        for copy in fetched:
            copy.start()
        for copy in fetched:
            copy.wait()
        c_ref, d_ref, h_ref, s_ref, band_ref, local_ref = held
        coeff_ref, stacked_ref, two_ref, four_ref, near_ref = outs
        for i in range(rows // BLK):
            at = slice(i * BLK, (i + 1) * BLK)
            for j in range(cols // BLK):
                block = c_ref[at, j * BLK : (j + 1) * BLK]
                block = jnp.where(local_ref[i, j] != 0, block, jnp.zeros_like(block))
                for ref in (coeff_ref, stacked_ref, two_ref, four_ref):
                    ref[at, j * BLK : (j + 1) * BLK] = block
            stacked_ref[at, cols:] = d_ref[at, :]
            for j in range(reach * rows // BLK):
                step, within = divmod(j * BLK, rows)
                for m, ref in enumerate((h_ref, s_ref)):
                    block = ref[at, j * BLK : (j + 1) * BLK]
                    block = jnp.where(band_ref[i, j] != 0, block, jnp.zeros_like(block))
                    start = cols + m * rows + within
                    if step == 0:
                        near_ref[at, start - cols : start - cols + BLK] = block

                        @pl.when(who_ref[0] != 0)
                        def _(block=block, start=start, at=at):
                            two_ref[at, start : start + BLK] = block

                    if step == 1:
                        two_ref[at, start + pack - cols : start + pack - cols + BLK] = block
                    if step == 2:
                        four_ref[at, start : start + BLK] = block

                        @pl.when(who_ref[0] == 0)
                        def _(block=block, start=start, at=at):
                            two_ref[at, start : start + BLK] = block

                    if step == 3:
                        four_ref[at, start + pack - cols : start + pack - cols + BLK] = block

    def like(*shape):
        return jax.ShapeDtypeStruct(shape, coeffs.dtype)

    sources = (coeffs, direction, ham_band, ovl_band, band_mask, local_mask)
    vmem = pl.BlockSpec(memory_space=pltpu.VMEM)
    wide = pack + 2 * rows
    return pl.pallas_call(
        kernel,
        out_shape=(
            like(rows, cols), like(rows, 2 * cols), like(rows, wide), like(rows, wide), like(rows, 2 * rows),
        ),
        in_specs=[pl.BlockSpec(memory_space=pltpu.SMEM)]
        + [pl.BlockSpec(memory_space=pltpu.HBM)] * len(sources),
        out_specs=(vmem,) * 5,
        scratch_shapes=[pltpu.VMEM(source.shape, source.dtype) for source in sources[:4]]
        + [pltpu.SMEM(source.shape, source.dtype) for source in sources[4:]]
        + [pltpu.SemaphoreType.DMA((len(sources),))],
        compiler_params=pltpu.CompilerParams(vmem_limit_bytes=60 * 2**20),
        cost_estimate=pl.CostEstimate(flops=0, bytes_accessed=20 * rows * wide, transcendentals=0),
    )(who, *sources)


def summed_copies(parts, scale, *others):
    def kernel(parts_ref, *refs):
        total = parts_ref[0]
        for i in range(1, parts.shape[0]):
            total = total + parts_ref[i]
        total = total * scale
        for i in range(parts.shape[0]):
            refs[-1][i] = total

    return pl.pallas_call(
        kernel,
        out_shape=jax.ShapeDtypeStruct(parts.shape, parts.dtype),
        in_specs=[pl.BlockSpec(memory_space=pltpu.VMEM)]
        + [pl.BlockSpec(memory_space=pl.ANY)] * len(others),
        out_specs=pl.BlockSpec(memory_space=pltpu.VMEM),
        compiler_params=pltpu.CompilerParams(vmem_limit_bytes=16 * 2**20),
        cost_estimate=pl.CostEstimate(flops=parts.size, bytes_accessed=8 * parts.size, transcendentals=0),
    )(parts, *others)


def finished(who, half, other_half, own, others, direction, local_mask):
    rows, wide = own.shape
    cols = wide // 2
    mid = rows // 2

    def split(value):
        high = value.astype(jnp.bfloat16)
        return high, (value - high.astype(jnp.float32)).astype(jnp.bfloat16)

    def kernel(who_ref, half_ref, far_ref, own_ref, *refs):
        other_refs, (d_ref, local_ref, grad_ref, line_ref, high_ref, low_ref) = refs[:6], refs[6:]
        for k in range(2):
            for base, ref in ((2 * who_ref[0], half_ref), (2 - 2 * who_ref[0], far_ref)):
                high, low = split(ref[k])
                high_ref[base + k] = high
                low_ref[base + k] = low
        line = jnp.zeros((1, cols), jnp.float32)
        for i in range(2):
            at = slice(i * mid, (i + 1) * mid)
            total = jnp.zeros((mid, cols), jnp.float32)
            for b in range(4):
                held = own_ref[at, :] if b == 0 else other_refs[2 * b - 2 + i][...]
                high, low = split(held)
                for x in range(2):
                    part = slice(x * cols, (x + 1) * cols)
                    for left, right in ((high, high_ref), (high, low_ref), (low, high_ref)):
                        total = total + jnp.dot(
                            left[:, part], right[b, :, part], preferred_element_type=jnp.float32
                        )
            grad = 4.0 * own_ref[at, cols:] - 2.0 * total
            for j in range(cols // BLK):
                side = slice(j * BLK, (j + 1) * BLK)
                block = grad[:, side]
                grad_ref[at, side] = jnp.where(local_ref[i, j] != 0, block, jnp.zeros_like(block))
            line = line + jnp.sum(
                d_ref[at, :].astype(jnp.float32) * grad_ref[at, :], axis=0, keepdims=True
            )
        line_ref[...] = line

    smem, vmem = pl.BlockSpec(memory_space=pltpu.SMEM), pl.BlockSpec(memory_space=pltpu.VMEM)
    return pl.pallas_call(
        kernel,
        out_shape=(
            jax.ShapeDtypeStruct((rows, cols), jnp.float32), jax.ShapeDtypeStruct((1, cols), jnp.float32),
        ),
        in_specs=[smem] + [vmem] * 10 + [smem],
        out_specs=(vmem, vmem),
        scratch_shapes=[pltpu.VMEM((4, cols, wide), jnp.bfloat16)] * 2,
        compiler_params=pltpu.CompilerParams(vmem_limit_bytes=24 * 2**20),
        cost_estimate=pl.CostEstimate(
            flops=24 * rows * wide * cols, bytes_accessed=20 * rows * wide * 4, transcendentals=0
        ),
    )(who, half, other_half, own, *others, direction, local_mask)


def on_device(coeffs, direction, ham_diag, ovl_diag, ham_band, ovl_band, band_mask, local_mask):
    rows = coeffs.shape[0]
    cols = coeffs.shape[1]
    basis_total = rows * lax.axis_size(BASIS)
    core = lax.axis_index("c")
    first_core = core == 0
    coeff, stacked, sent_2, sent_4, nearest = prepared(
        jnp.stack([core]).astype(jnp.int32),
        coeffs, direction, ham_band, ovl_band, band_mask, local_mask,
    )

    ahead_2 = shifted(stacked, -2)
    ahead_4 = shifted(stacked, -4)
    behind_2 = shifted(sent_2, 2)
    behind_4 = shifted(sent_4, 4)
    place = lax.axis_index("orb")
    every_coeff = lax.all_gather(coeff, "orb", axis=0)

    def peer(g):
        return lax.dynamic_index_in_dim(every_coeff, (place + g) % SIZES["orb"], 0, keepdims=False)

    near_peers = [peer(2 * core + k) for k in range(2)]
    pack = cols + 2 * rows
    wanted = [(place + 2 - 2 * core + k) % SIZES["orb"] for k in range(2)]
    who = jnp.stack([core] + wanted).astype(jnp.int32)
    crossed = swapped(
        packed(who, coeff, nearest, behind_2, behind_4, stacked, ahead_2, ahead_4, every_coeff), "c"
    )
    odd_behind = crossed[:, : 2 * pack]
    odd_ahead = crossed[:, 2 * pack : 2 * pack + 4 * cols]
    gram_left = jnp.concatenate(
        [
            jnp.concatenate(near_peers, axis=1),
            crossed[:, 2 * pack + 4 * cols :],
        ],
        axis=0,
    )

    band_full = expand_mask(band_mask).astype(jnp.bfloat16)
    upright = [
        jnp.concatenate(
            [(band * band_full)[:, k * rows : (k + 1) * rows] for band in (ham_band, ovl_band)], axis=0
        )
        for k in range(ham_band.shape[1] // rows)
    ]

    forward = plain_dot(jnp.concatenate([ham_diag, ovl_diag], axis=0), stacked)
    forward = forward + plain_dot(upright[1], ahead_2)
    forward = forward + plain_dot(upright[3], ahead_4)
    forward = forward + plain_dot(upright[0], odd_ahead[:, : 2 * cols])
    forward = forward + plain_dot(upright[2], odd_ahead[:, 2 * cols :])
    back = dot_left(jnp.concatenate([ham_diag, ovl_diag], axis=1), coeff)
    back = back + dot_left(behind_2[:, pack:], behind_2[:, :cols])
    back = back + dot_left(behind_4[:, pack:], behind_4[:, :cols])
    back = back + dot_left(odd_behind[:, cols:pack], odd_behind[:, :cols])
    back = back + dot_left(odd_behind[:, pack + cols :], odd_behind[:, pack : pack + cols])
    ham_c = forward[:rows, :cols] + back[:rows]
    ovl_c = forward[rows:, :cols] + back[rows:] + coeff.astype(jnp.float32)
    both_c = jnp.concatenate([ham_c, ovl_c], axis=1)

    dir_f = direction.astype(jnp.float32)
    ham_line = 2.0 * jnp.sum(dir_f * forward[:rows, cols:], axis=0)
    ovl_line = jnp.sum(dir_f * (2.0 * forward[rows:, cols:] + dir_f), axis=0)

    swapped_c = jnp.concatenate([ovl_c, ham_c], axis=1)
    mid = rows // 2
    next_top, last_bottom = over_orb(swapped_c[:mid], -1), over_orb(swapped_c[mid:], 1)
    next_bottom, last_top = over_orb(swapped_c[mid:], -1), over_orb(swapped_c[:mid], 1)
    other_c = swapped(both_c, "c")

    partial = dot_left(
        gram_left.astype(jnp.float32), jnp.concatenate([both_c, other_c], axis=0), HIGH
    )
    chip_axes = ("y", "z", "x")
    chips = lax.axis_size(chip_axes)
    parts = lax.all_to_all(
        partial.reshape(chips, 2 * cols // chips, 2 * cols), chip_axes, 0, 0
    )
    copies = summed_copies(
        parts, 1.0 / basis_total, next_top[:8, :BLK], last_bottom[:8, :BLK]
    )
    top = over_orb(next_top, -1)
    bottom = over_orb(last_bottom, 1)
    half = lax.all_to_all(copies, chip_axes, 0, 0).reshape(2, cols, 2 * cols)
    half, top, bottom, next_bottom, last_top = lax.optimization_barrier(
        (half, top, bottom, next_bottom, last_top)
    )
    other_half = swapped(half, "c")
    gradient, grad_line = finished(
        jnp.stack([core]).astype(jnp.int32), half, other_half, swapped_c,
        [next_top, next_bottom, top, bottom, last_top, last_bottom], direction, local_mask,
    )
    lines = jnp.stack([ham_line, ovl_line, grad_line[0]], axis=0)
    lines = lines + swapped(lines, "c")
    copies = jnp.broadcast_to(lines.reshape(1, -1, BLK), (chips, lines.size // BLK, BLK))
    every_line = lax.all_to_all(copies, chip_axes, 0, 0)
    line_terms = jnp.sum(every_line, axis=0).reshape(lines.shape) * (1.0 / math.sqrt(basis_total))
    return (gradient, line_terms)


def solution(mesh):
    fine = Mesh(mesh.devices.reshape(tuple(SIZES.values())), tuple(SIZES))
    placed = (P(BASIS, "orb"), P(BASIS, "orb")) + (P(BASIS, None),) * 5 + (P(BASIS, "orb"),)
    return jax.shard_map(
        on_device,
        mesh=fine,
        in_specs=placed,
        out_specs=(P(BASIS, "orb"), P(None, "orb")),
        check_vma=False,
    )
```
